32 devices in a mesh: aa: 8 (over z, core), ba: 4 (over y, x).
Axes of the slice: x: 2, y: 2, z: 4, core: 2. Of those that a mesh axis runs over, the one named last changes fastest.
Arguments:
- right_sides: bfloat16 [32768, 512], P(('aa', 'ba')), may hold values from -6 to 6
- point_order: int32 [32, 1024], P(('aa', 'ba')), may hold values from 0 to 1023, each once within a row
- skeleton: int32 [32, 128], P(('aa', 'ba')), may hold values from 0 to 1023, as said below
- leaf_inverse: bfloat16 [32768, 1024], P(('aa', 'ba')), may hold values from -1 to 3.5
- leaf_basis: bfloat16 [32768, 128], P(('aa', 'ba')), may hold values from -0.1875 to 0.1875
- group_core: bfloat16 [4096, 512], P(('aa', 'ba')), may hold values from -1 to 2, as said below
- transfer: float32 [4096, 128], P(('aa', 'ba')), may hold values from -0.5 to 0.5
- top_core: bfloat16 [1024, 1024], P(('aa', 'ba')), may hold values from -1 to 2
Outputs:
- solution: bfloat16 [32768, 512], P(('aa', 'ba'))
The draws below stay inside these ranges and needn't reach their ends.
Inputs may be any that keep to these rules, and one draw needn't show every extreme that they name: `skeleton`: each row holds 128 different indices in increasing order. `group_core`: each group's block of 512 rows is symmetric.
All inputs are finite; a program needn't handle non-finite values.
Results may differ from the reference program's by a relative error of at most 0.014.
Values may be sent and summed in bfloat16 or wider, within the bound.
No kernel may reach another device: no remote copies, remote signals or barrier semaphores. Data moves between devices by JAX's collectives and lax.ppermute only.
A program may use at most 64 MiB of HBM per device.

```python
import math
import jax
import jax.numpy as jnp
from jax import lax

LEAF = 1024
RANK = 128
RHS = 512
LEAVES = 32
POINTS = 32768
GROUP = 512
TOP = 1024
N_AA = 8
N_BA = 4


def draw_skeleton(key, part):
    leaf_keys = jax.random.split(key, LEAVES)
    shuffled = jax.vmap(lambda leaf_key: jax.random.permutation(leaf_key, LEAF))(leaf_keys)
    return jnp.sort(shuffled[:, :RANK], axis=1).astype(jnp.int32)


def draw_leaf_inverse(key, part):
    diag_key, off_key = jax.random.split(jax.random.fold_in(key, 11))
    diagonal = jnp.exp(jax.random.uniform(diag_key, (LEAVES, LEAF), jnp.float32, math.log(0.5), math.log(2.0)))
    spread = jax.random.truncated_normal(off_key, -4.0, 4.0, (LEAVES, LEAF, LEAF), jnp.float32) * (0.5 / math.sqrt(LEAF))
    position = jnp.arange(LEAF)
    matrix = spread.at[:, position, position].add(diagonal)
    return matrix.reshape(LEAVES * LEAF, LEAF).astype(jnp.bfloat16)


def core_matrix(key, groups, order, scale):
    diag_key, off_key = jax.random.split(key)
    diagonal = jnp.exp(jax.random.uniform(diag_key, (groups, order), jnp.float32, math.log(0.3), 0.0))
    spread = jax.random.truncated_normal(off_key, -4.0, 4.0, (groups, order, order), jnp.float32)
    matrix = (spread + jnp.swapaxes(spread, 1, 2)) * (0.6 / math.sqrt(2.0 * order))
    position = jnp.arange(order)
    matrix = matrix.at[:, position, position].add(diagonal)
    return matrix * scale


def draw_group_core(key, part):
    matrix = core_matrix(jax.random.fold_in(key, 23), TOP // RANK, GROUP, 1.0)
    return matrix.reshape(TOP // RANK * GROUP, GROUP).astype(jnp.bfloat16)


def draw_top_core(key, part):
    matrix = core_matrix(jax.random.fold_in(key, 37), 1, TOP, 1.0 / math.sqrt(GROUP // RANK))
    return matrix.reshape(TOP, TOP).astype(jnp.bfloat16)


def block_scale(own_key, shape, cuts, low, high):
    def one(axis_at, shards_of):
        draws = jax.random.uniform(jax.random.fold_in(jax.random.fold_in(own_key, 6), axis_at), (shards_of,), jnp.float32, low / len(cuts), high / len(cuts))
        return jnp.repeat(jnp.exp(draws), shape[axis_at] // shards_of).reshape((-1,) + (1,) * (len(shape) - axis_at - 1))

    factor_of = one(*cuts[0])
    for cut in cuts[1:]:
        factor_of = factor_of * one(*cut)
    return factor_of


def gaussian(own_key, dims, deviation, bound, pieces=(), kind=jnp.bfloat16):
    array = deviation * jax.random.normal(own_key, dims, jnp.float32)
    if pieces:
        array = array * block_scale(own_key, dims, pieces, -0.22, 0.18)
    return jnp.clip(array, -bound, bound).astype(kind)


def setup_inputs(seed: int = 0) -> dict:
    key_list = jax.random.split(jax.random.key(seed), 9)
    right_sides = gaussian(key_list[0], (POINTS, RHS), 1.0, 6.0, ((0, 32),))
    point_order = jax.vmap(lambda own: jax.random.permutation(own, LEAF))(jax.random.split(key_list[1], LEAVES)).reshape((LEAVES, LEAF)).astype(jnp.int32)
    skeleton = draw_skeleton(jax.random.fold_in(key_list[8], 71), 0)
    leaf_inverse = draw_leaf_inverse(jax.random.fold_in(key_list[8], 71), 0)
    leaf_basis = gaussian(key_list[4], (POINTS, RANK), LEAF ** -0.5, 0.1875, ((0, 32),))
    group_core = draw_group_core(jax.random.fold_in(key_list[8], 71), 0)
    transfer = gaussian(key_list[6], (LEAVES * RANK, RANK), RANK ** -0.5, 0.5, ((0, 32),), jnp.float32)
    top_core = draw_top_core(jax.random.fold_in(key_list[8], 71), 0)
    return {"right_sides": right_sides, "point_order": point_order, "skeleton": skeleton, "leaf_inverse": leaf_inverse, "leaf_basis": leaf_basis, "group_core": group_core, "transfer": transfer, "top_core": top_core}


def rounded(values):
    return lax.optimization_barrier(values.astype(jnp.bfloat16)).astype(jnp.float32)


def leaf_up(leaf_args):
    sides, ordering, skel_rows, inverse, leaf_base = leaf_args
    ordered = sides[ordering].astype(jnp.float32)
    applied = jnp.dot(inverse.astype(jnp.float32), ordered)
    coeffs = jnp.dot(leaf_base.astype(jnp.float32).T, rounded(applied)) + applied[skel_rows]
    return applied, coeffs


def leaf_down(leaf_args):
    applied, leaf_correction, ordering, skel_rows, inverse, leaf_base = leaf_args
    expanded = jnp.dot(leaf_base.astype(jnp.float32), rounded(leaf_correction))
    expanded = expanded.at[skel_rows].add(leaf_correction)
    solved = applied - jnp.dot(inverse.astype(jnp.float32), rounded(expanded))
    placed = jnp.zeros(solved.shape, jnp.bfloat16)
    return placed.at[ordering].set(solved.astype(jnp.bfloat16))


def reference(right_sides, point_order, skeleton, leaf_inverse, leaf_basis, group_core, transfer, top_core):
    side_leaves = right_sides.reshape(LEAVES, LEAF, RHS)
    inverse_leaves = leaf_inverse.reshape(LEAVES, LEAF, LEAF)
    basis_leaves = leaf_basis.reshape(LEAVES, LEAF, RANK)
    applied, coeffs = lax.map(leaf_up, (side_leaves, point_order, skeleton, inverse_leaves, basis_leaves))
    cores = group_core.reshape(N_AA, GROUP, GROUP).astype(jnp.float32)
    stacked = rounded(coeffs.reshape(N_AA, GROUP, RHS))
    level_one = jnp.einsum("agh,ahc->agc", cores, stacked, precision=lax.Precision.HIGHEST)
    level_one = level_one.reshape(LEAVES, RANK, RHS)
    remainder = coeffs - level_one
    transfer_leaves = transfer.reshape(LEAVES, RANK, RANK)
    partial_value = jnp.einsum("lrs,lrc->lsc", transfer_leaves, remainder, precision=lax.Precision.HIGHEST)
    group_coeffs = partial_value.reshape(N_AA, N_BA, RANK, RHS).sum(axis=1)
    top = jnp.dot(top_core.astype(jnp.float32), rounded(group_coeffs.reshape(TOP, RHS)), precision=lax.Precision.HIGHEST)
    top_leaves = jnp.broadcast_to(top.reshape(N_AA, 1, RANK, RHS), (N_AA, N_BA, RANK, RHS)).reshape(LEAVES, RANK, RHS)
    correction = level_one + jnp.einsum("lrs,lsc->lrc", transfer_leaves, top_leaves, precision=lax.Precision.HIGHEST)
    solved = lax.map(leaf_down, (applied, correction, point_order, skeleton, inverse_leaves, basis_leaves))
    return solved.reshape(POINTS, RHS)
```

```python
import functools

import jax
import jax.numpy as jnp
from jax import lax
from jax.experimental import pallas as pl
from jax.experimental.pallas import tpu as pltpu
from jax.sharding import PartitionSpec as P

BF = jnp.bfloat16
F32 = jnp.float32
NN = (((1,), (0,)), ((), ()))
NT = (((1,), (1,)), ((), ()))
TN = (((0,), (0,)), ((), ()))


def dot(a, b, dims=NN):
    return lax.dot_general(a, b, dims, preferred_element_type=F32)


def partners(n, k):
    half = (n - 2) // 2
    return [(k - 1 + j) % (n - 1) + 1 for j in range(1, half + 1)]


def column_of(row, count):
    wide = jnp.broadcast_to(row.astype(F32), (count, row.shape[1]))
    return wide.T.astype(jnp.int32)


def order_rows(order, size):
    return jnp.where(
        lax.broadcasted_iota(jnp.int32, (size, size), 0) == order, 1.0, 0.0
    ).astype(BF)


def basis_pair(skel, basis):
    points, rank = basis.shape
    ones = jnp.where(
        lax.broadcasted_iota(jnp.int32, (points, rank), 0) == skel, 1.0, 0.0
    ).astype(BF)
    return jnp.concatenate([basis, ones], axis=1)


def front_kernel(n, order_ref, skel_ref, sides_ref, inverse_ref, basis_ref, core_ref, transfer_ref, top_ref, *rest):
    messages, (own_ref, held, coeffs, sems) = rest[: n - 1], rest[n - 1 :]
    me = lax.axis_index("ba")
    points, rank = basis_ref.shape
    pieces = sems.shape[0]
    rows = points // pieces
    copies = [
        pltpu.make_async_copy(
            inverse_ref.at[pl.ds(j * rows, rows)], held.at[pl.ds(j * rows, rows)], sems.at[j]
        )
        for j in range(pieces)
    ]
    for copy in copies:
        copy.start()
    share = own_ref.shape[0]
    transfer = transfer_ref[...].astype(BF)
    groups = top_ref.shape[1] // rank
    top = top_ref[...].astype(F32)
    top = jnp.concatenate([top[:, g * rank : (g + 1) * rank] for g in range(groups)], axis=0).astype(BF)
    for k in range(1, n):
        out = messages[k - 1]
        at = share
        out[at : at + rank, :] = transfer
        at += rank
        for m in [k] + partners(n, k):
            block = me ^ (k ^ m)
            out[at : at + rank, :] = core_ref[:, pl.ds(pl.multiple_of(block * rank, rank), rank)]
            at += rank
        out[at:, :] = top
    placed = order_rows(order_ref[...], points)
    pair = basis_pair(skel_ref[...], basis_ref[...])
    both = None
    for j, copy in enumerate(copies):
        copy.wait()
        part = dot(pair[j * rows : (j + 1) * rows], held[j * rows : (j + 1) * rows, :], TN)
        both = part if both is None else both + part
    up = (both[:rank] + both[rank:]).astype(BF)
    up = dot(up, placed, NT).astype(BF)
    coeffs[...] = dot(up, sides_ref[...]).T.astype(BF)
    own_ref[...] = coeffs[pl.ds(pl.multiple_of(me * share, share), share), :]
    for k in range(1, n):
        messages[k - 1][0:share, :] = coeffs[pl.ds(pl.multiple_of((me ^ k) * share, share), share), :]


def leaf_kernel(order_ref, skel_ref, sides_ref, inverse_ref, basis_ref, applied_ref, down_ref):
    points, rank = basis_ref.shape
    order = order_ref[...]
    column = column_of(order, 128)
    lanes = lax.broadcasted_iota(jnp.int32, (points, 128), 1)
    gather = jnp.concatenate(
        [jnp.where(column == lanes + j * 128, 1.0, 0.0).astype(BF) for j in range(points // 128)], axis=1
    )
    ordered = dot(gather, sides_ref[...]).astype(BF)
    applied = dot(inverse_ref[...], ordered).astype(BF)
    placed = order_rows(order, points)
    applied_ref[...] = dot(placed, applied).astype(BF)
    both = dot(inverse_ref[...], basis_pair(skel_ref[...], basis_ref[...]))
    down = (both[:, :rank] + both[:, rank:]).astype(BF)
    down_ref[...] = dot(placed, down).astype(BF)


def group_kernel(n, own_ref, core_ref, transfer_ref, *rest):
    messages, (level_ref, group_ref) = rest[: n - 1], rest[n - 1 :]
    me = lax.axis_index("ba")
    share, rank = own_ref.shape
    core = {}
    for m in range(n):
        core[0, m] = core_ref[:, pl.ds(pl.multiple_of((me ^ m) * rank, rank), rank)]
    for k in range(1, n):
        at = share + rank
        for m in [k] + partners(n, k):
            core[k, m] = messages[k - 1][at : at + rank, :]
            at += rank
    coeffs = [own_ref[...]] + [msg[0:share, :] for msg in messages]
    transfers = [transfer_ref[...].astype(BF)] + [msg[share : share + rank, :] for msg in messages]
    total = None
    for k in range(n):
        level = None
        for m in range(n):
            term = dot(coeffs[m], core[m, k]) if (m, k) in core else dot(coeffs[m], core[k, m], NT)
            level = term if level is None else level + term
        level_ref[:, k * rank : (k + 1) * rank] = level
        rest_of = (coeffs[k].astype(F32) - level).astype(BF)
        term = dot(rest_of, transfers[k])
        total = term if total is None else total + term
    group_ref[...] = total.astype(BF)


def top_rows_kernel(n, groups, top_ref, transfer_ref, *rest):
    messages, (rows_ref, transfers_ref, held) = rest[: n - 1], rest[n - 1 :]
    me = lax.axis_index("ba")
    mine = lax.axis_index("aa")
    rank = transfer_ref.shape[0]
    part = top_ref.shape[0]
    transfers_ref[0:rank, :] = transfer_ref[...].astype(BF)
    held[pl.ds(pl.multiple_of(me * part, part), part), :] = top_ref[...].astype(F32)
    for k in range(1, n):
        msg = messages[k - 1]
        share = msg.shape[0] - (groups * part + rank * (2 + len(partners(n, k))))
        transfers_ref[k * rank : (k + 1) * rank, :] = msg[share : share + rank, :]
        tail = msg[msg.shape[0] - groups * part :, :].astype(F32)
        for g in range(groups):
            held[pl.ds(pl.multiple_of((me ^ k) * part, part), part), g * rank : (g + 1) * rank] = tail[
                g * part : (g + 1) * part
            ]
    for m in range(groups):
        rows_ref[:, m * rank : (m + 1) * rank] = held[
            :, pl.ds(pl.multiple_of((mine ^ m) * rank, rank), rank)
        ].astype(BF)


def top_kernel(n, groups, rows_ref, transfers_ref, level_ref, *rest):
    pieces, outs = rest[:groups], rest[groups:]
    rank = transfers_ref.shape[1]
    stacked = jnp.concatenate([piece[...] for piece in pieces], axis=1)
    top = dot(stacked, rows_ref[...], NT).astype(BF)
    correction = (level_ref[...] + dot(top, transfers_ref[...], NT)).astype(BF)
    for k in range(n):
        outs[k][...] = correction[:, k * rank : (k + 1) * rank]


def final_kernel(n, applied_ref, down_ref, *rest):
    pieces, (out_ref, correction) = rest[:n], rest[n:]
    me = lax.axis_index("ba")
    share = pieces[0].shape[0]
    for k in range(n):
        correction[pl.ds(pl.multiple_of((me ^ k) * share, share), share), :] = pieces[k][...]
    out_ref[...] = (applied_ref[...].astype(F32) - dot(down_ref[...], correction[...], NT)).astype(BF)


def shape(dims, kind=BF):
    return jax.ShapeDtypeStruct(dims, kind)


def call(body, outs, in_specs=None, scratch=(), flops=0, moved=0):
    limit = pltpu.CompilerParams(vmem_limit_bytes=48 * 1024 * 1024)
    extra = {} if in_specs is None else {"in_specs": in_specs}
    return pl.pallas_call(
        body,
        out_shape=outs,
        scratch_shapes=list(scratch),
        compiler_params=limit,
        cost_estimate=pl.CostEstimate(flops=flops, bytes_accessed=moved, transcendentals=0),
        **extra,
    )


def shards(n, groups, sides, order, skel, inverse, basis, core, transfer, top):
    points, cols = sides.shape
    rank = basis.shape[1]
    share = cols // n
    part = top.shape[0]
    vmem = pl.BlockSpec(memory_space=pltpu.VMEM)
    sizes = [share + rank * (2 + len(partners(n, k))) + groups * part for k in range(1, n)]
    front = call(
        functools.partial(front_kernel, n),
        [shape((size, rank)) for size in sizes] + [shape((share, rank))],
        in_specs=[vmem, vmem, vmem, pl.BlockSpec(memory_space=pl.ANY)] + [vmem] * 4,
        scratch=[
            pltpu.VMEM((points, points), BF),
            pltpu.VMEM((cols, rank), BF),
            pltpu.SemaphoreType.DMA((2,)),
        ],
        flops=2 * rank * points * (3 * points + cols),
        moved=2 * points * (points + cols + rank),
    )(order, skel, sides, inverse, basis, core, transfer, top)
    own = front[n - 1]
    received = [
        lax.ppermute(front[k - 1], "ba", [(i, i ^ k) for i in range(n)]) for k in range(1, n)
    ]
    applied, down = call(
        leaf_kernel,
        [shape((points, cols)), shape((points, rank))],
        flops=2 * points * points * (3 * cols + 3 * rank),
        moved=2 * points * (points + 2 * cols + 2 * rank),
    )(order, skel, sides, inverse, basis)
    level, group = call(
        functools.partial(group_kernel, n),
        [shape((share, n * rank), F32), shape((share, rank))],
        flops=2 * share * n * rank * (n + 1) * rank,
        moved=4 * share * n * rank,
    )(own, core, transfer, *received)
    rows, transfers = call(
        functools.partial(top_rows_kernel, n, groups),
        [shape((rank, groups * rank)), shape((n * rank, rank))],
        scratch=[pltpu.VMEM((rank, groups * rank), F32)],
        moved=4 * rank * groups * rank,
    )(top, transfer, *received)
    pieces = {0: group}
    for m in range(2, groups, 2):
        pieces[m] = lax.ppermute(group, "aa", [(i, i ^ m) for i in range(groups)])
    for m in range(0, groups, 2):
        pieces[m + 1] = lax.ppermute(pieces[m], "aa", [(i, i ^ 1) for i in range(groups)])
    corrections = call(
        functools.partial(top_kernel, n, groups),
        [shape((share, rank))] * n,
        flops=2 * share * rank * (groups + n) * rank,
        moved=4 * share * n * rank,
    )(rows, transfers, level, *[pieces[m] for m in range(groups)])
    back = [corrections[0]] + [
        lax.ppermute(corrections[k], "ba", [(i, i ^ k) for i in range(n)]) for k in range(1, n)
    ]
    return call(
        functools.partial(final_kernel, n),
        shape((points, cols)),
        scratch=[pltpu.VMEM((cols, rank), BF)],
        flops=2 * points * cols * rank,
        moved=4 * points * cols,
    )(applied, down, *back)


def solution(mesh):
    spec = P(("aa", "ba"), None)
    return jax.shard_map(
        functools.partial(shards, mesh.shape["ba"], mesh.shape["aa"]),
        mesh=mesh,
        in_specs=(spec,) * 8,
        out_specs=spec,
        check_vma=False,
    )
```

```python
import functools

import jax
import jax.numpy as jnp
from jax import lax
from jax.experimental import pallas as pl
from jax.experimental.pallas import tpu as pltpu
from jax.sharding import PartitionSpec as P

BF = jnp.bfloat16
F32 = jnp.float32
NN = (((1,), (0,)), ((), ()))
NT = (((1,), (1,)), ((), ()))
TN = (((0,), (0,)), ((), ()))


def dot(a, b, dims=NN):
    return lax.dot_general(a, b, dims, preferred_element_type=F32)


def partners(n, k):
    half = (n - 2) // 2
    return [(k - 1 + j) % (n - 1) + 1 for j in range(1, half + 1)]


def column_of(row, count):
    wide = jnp.broadcast_to(row.astype(F32), (count, row.shape[1]))
    return wide.T.astype(jnp.int32)


def order_rows(order, size):
    return jnp.where(
        lax.broadcasted_iota(jnp.int32, (size, size), 0) == order, 1.0, 0.0
    ).astype(BF)


def basis_pair(skel, basis):
    points, rank = basis.shape
    ones = jnp.where(
        lax.broadcasted_iota(jnp.int32, (points, rank), 0) == skel, 1.0, 0.0
    ).astype(BF)
    return jnp.concatenate([basis, ones], axis=1)


def fetch(sources, sems):
    copies = [pltpu.make_async_copy(src, dst, sems.at[j]) for j, (src, dst) in enumerate(sources)]
    for copy in copies:
        copy.start()
    return copies


def pieces_of(ref, count):
    rows = ref.shape[0] // count
    return [ref.at[pl.ds(j * rows, rows)] for j in range(count)]


PIECES = 4


def front_kernel(n, order_hbm, skel_hbm, sides_hbm, inverse_hbm, basis_hbm, core_hbm, transfer_hbm, top_hbm, *rest):
    messages, (own_ref, top_ref, order_ref, skel_ref, sides_ref, inverse_ref, basis_ref, core_ref, transfer_ref, coeffs, sems) = (
        rest[: n - 1],
        rest[n - 1 :],
    )
    me = lax.axis_index("ba")
    points, rank = basis_ref.shape
    rows = points // PIECES
    copies = fetch(
        [(skel_hbm, skel_ref), (basis_hbm, basis_ref), (order_hbm, order_ref)]
        + list(zip(pieces_of(inverse_hbm, PIECES), pieces_of(inverse_ref, PIECES)))
        + [(sides_hbm, sides_ref), (core_hbm, core_ref), (transfer_hbm, transfer_ref), (top_hbm, top_ref)],
        sems,
    )
    share = coeffs.shape[0] // n
    for copy in copies[:3]:
        copy.wait()
    pair = basis_pair(skel_ref[...], basis_ref[...])
    placed = order_rows(order_ref[...], points)
    both = None
    for j in range(PIECES):
        copies[3 + j].wait()
        part = dot(pair[j * rows : (j + 1) * rows], inverse_ref[j * rows : (j + 1) * rows, :], TN)
        both = part if both is None else both + part
    up = (both[:rank] + both[rank:]).astype(BF)
    up = dot(up, placed, NT).astype(BF)
    for copy in copies[3 + PIECES :]:
        copy.wait()
    coeffs[...] = dot(up, sides_ref[...]).T.astype(BF)
    transfer = transfer_ref[...].astype(BF)

    def block(m):
        return core_ref[:, pl.ds(pl.multiple_of((me ^ m) * rank, rank), rank)]

    for k in range(n):
        out = own_ref if k == 0 else messages[k - 1]
        out[0:share, :] = coeffs[pl.ds(pl.multiple_of((me ^ k) * share, share), share), :]
        out[share : share + rank, :] = transfer
        at = share + rank
        for m in range(n) if k == 0 else [0] + [k ^ m for m in partners(n, k)]:
            out[at : at + rank, :] = block(m)
            at += rank


def applied_kernel(order_hbm, sides_hbm, inverse_hbm, after, applied_ref, order_ref, sides_ref, inverse_ref, sems):
    del after
    points = sides_ref.shape[0]
    rows = points // PIECES
    copies = fetch(
        [(order_hbm, order_ref), (sides_hbm, sides_ref)]
        + list(zip(pieces_of(inverse_hbm, PIECES), pieces_of(inverse_ref, PIECES))),
        sems,
    )
    copies[0].wait()
    order = order_ref[...]
    column = column_of(order, 128)
    lanes = lax.broadcasted_iota(jnp.int32, (points, 128), 1)
    gather = jnp.concatenate(
        [jnp.where(column == lanes + j * 128, 1.0, 0.0).astype(BF) for j in range(points // 128)], axis=1
    )
    copies[1].wait()
    ordered = dot(gather, sides_ref[...]).astype(BF)
    parts = []
    for j in range(PIECES):
        copies[2 + j].wait()
        parts.append(dot(inverse_ref[j * rows : (j + 1) * rows, :], ordered).astype(BF))
    applied_ref[...] = dot(order_rows(order, points), jnp.concatenate(parts, axis=0)).astype(BF)


def down_kernel(order_hbm, skel_hbm, inverse_hbm, basis_hbm, after, down_ref, order_ref, skel_ref, inverse_ref, basis_ref, sems):
    del after
    points, rank = basis_ref.shape
    rows = points // PIECES
    copies = fetch(
        [(order_hbm, order_ref), (skel_hbm, skel_ref), (basis_hbm, basis_ref)]
        + list(zip(pieces_of(inverse_hbm, PIECES), pieces_of(inverse_ref, PIECES))),
        sems,
    )
    for copy in copies[:3]:
        copy.wait()
    pair = basis_pair(skel_ref[...], basis_ref[...])
    placed = order_rows(order_ref[...], points)
    parts = []
    for j in range(PIECES):
        copies[3 + j].wait()
        both = dot(inverse_ref[j * rows : (j + 1) * rows, :], pair)
        parts.append((both[:, :rank] + both[:, rank:]).astype(BF))
    down_ref[...] = dot(placed, jnp.concatenate(parts, axis=0)).astype(BF)


def group_kernel(n, rank, after, top_ref, own_ref, *rest):
    del after
    messages, (level_ref, group_ref, top_out) = rest[: n - 1], rest[n - 1 :]
    share = level_ref.shape[0]
    core = {}
    for k in range(n):
        at = share + rank
        for m in range(n) if k == 0 else [k] + partners(n, k):
            core[k, m] = own_ref[at : at + rank, :] if k == 0 else messages[k - 1][at : at + rank, :]
            at += rank
    coeffs = [msg[0:share, :] for msg in (own_ref,) + messages]
    transfers = [msg[share : share + rank, :] for msg in (own_ref,) + messages]
    total = None
    for k in range(n):
        level = None
        for m in range(n):
            term = dot(coeffs[m], core[m, k]) if (m, k) in core else dot(coeffs[m], core[k, m], NT)
            level = term if level is None else level + term
        level_ref[:, k * rank : (k + 1) * rank] = level
        rest_of = (coeffs[k].astype(F32) - level).astype(BF)
        term = dot(rest_of, transfers[k])
        total = term if total is None else total + term
    group_ref[...] = total.astype(BF)
    top_out[...] = top_ref[...]


def top_rows_kernel(n, groups, *rest):
    tops, (rows_ref, held) = rest[:n], rest[n:]
    me = lax.axis_index("ba")
    mine = lax.axis_index("aa")
    part = tops[0].shape[0]
    rank = rows_ref.shape[0]
    for k in range(n):
        held[pl.ds(pl.multiple_of((me ^ k) * part, part), part), :] = tops[k][...].astype(F32)
    for m in range(groups):
        rows_ref[:, m * rank : (m + 1) * rank] = held[
            :, pl.ds(pl.multiple_of((mine ^ m) * rank, rank), rank)
        ].astype(BF)


def top_kernel(n, groups, rows_ref, level_ref, *rest):
    messages, pieces, outs = rest[:n], rest[n : n + groups], rest[n + groups :]
    share = level_ref.shape[0]
    rank = rows_ref.shape[0]
    stacked = jnp.concatenate([piece[...] for piece in pieces], axis=1)
    top = dot(stacked, rows_ref[...], NT).astype(BF)
    transfers = jnp.concatenate([msg[share : share + rank, :] for msg in messages], axis=0)
    correction = (level_ref[...] + dot(top, transfers, NT)).astype(BF)
    for k in range(n):
        outs[k][...] = correction[:, k * rank : (k + 1) * rank]


def final_kernel(n, applied_ref, down_ref, *rest):
    pieces, (out_hbm, correction, out_ref, sems) = rest[:n], rest[n:]
    me = lax.axis_index("ba")
    share = pieces[0].shape[0]
    for k in range(n):
        correction[pl.ds(pl.multiple_of((me ^ k) * share, share), share), :] = pieces[k][...]
    rows = out_ref.shape[0] // PIECES
    copies = []
    for j, (src, dst) in enumerate(zip(pieces_of(out_ref, PIECES), pieces_of(out_hbm, PIECES))):
        at = slice(j * rows, (j + 1) * rows)
        out_ref[at, :] = (
            applied_ref[at, :].astype(F32) - dot(down_ref[at, :], correction[...], NT)
        ).astype(BF)
        copies.append(pltpu.make_async_copy(src, dst, sems.at[j]))
        copies[-1].start()
    for copy in copies:
        copy.wait()


def shape(dims, kind=BF):
    return jax.ShapeDtypeStruct(dims, kind)


def call(body, outs, in_specs, out_specs=None, scratch=(), flops=0, moved=0):
    return pl.pallas_call(
        body,
        out_shape=outs,
        in_specs=in_specs,
        scratch_shapes=list(scratch),
        compiler_params=pltpu.CompilerParams(vmem_limit_bytes=48 * 1024 * 1024),
        cost_estimate=pl.CostEstimate(flops=flops, bytes_accessed=moved, transcendentals=0),
        **({} if out_specs is None else {"out_specs": out_specs}),
    )


def shards(n, groups, sides, order, skel, inverse, basis, core, transfer, top):
    points, cols = sides.shape
    rank = basis.shape[1]
    share = cols // n
    vmem = pl.BlockSpec(memory_space=pltpu.VMEM)
    hbm = pl.BlockSpec(memory_space=pltpu.HBM)
    unread = pl.BlockSpec(memory_space=pl.ANY)

    def like(array):
        return pltpu.VMEM(array.shape, array.dtype)

    def swap(array, axis, k):
        size = {"aa": groups, "ba": n}[axis]
        return lax.ppermute(array, axis, [(i, i ^ k) for i in range(size)])

    sizes = [share + rank * (2 + len(partners(n, k))) for k in range(1, n)] + [share + rank * (n + 1)]
    *messages, own, top_held = call(
        functools.partial(front_kernel, n),
        [shape((size, rank)) for size in sizes] + [shape(top.shape)],
        [hbm] * 8,
        scratch=[like(x) for x in (order, skel, sides, inverse, basis, core, transfer)]
        + [pltpu.VMEM((cols, rank), BF), pltpu.SemaphoreType.DMA((7 + PIECES,))],
        flops=2 * rank * points * (3 * points + cols),
        moved=2 * points * (points + cols + rank),
    )(order, skel, sides, inverse, basis, core, transfer, top)
    received = [swap(messages[k - 1], "ba", k) for k in range(1, n)]
    applied = call(
        applied_kernel,
        shape((points, cols)),
        [hbm] * 3 + [unread],
        scratch=[like(x) for x in (order, sides, inverse)] + [pltpu.SemaphoreType.DMA((2 + PIECES,))],
        flops=2 * points * points * 3 * cols,
        moved=2 * points * (points + 2 * cols),
    )(order, sides, inverse, own)
    level, group, top_held = call(
        functools.partial(group_kernel, n, rank),
        [shape((share, n * rank), F32), shape((share, rank)), shape(top.shape)],
        [unread] + [vmem] * (n + 1),
        flops=2 * share * n * rank * (n + 1) * rank,
        moved=4 * share * n * rank,
    )(applied, top_held, own, *received)
    pieces = {0: group}
    for m in range(2, groups, 2):
        pieces[m] = swap(group, "aa", m)
    tops = [top_held] + [swap(top_held, "ba", k) for k in range(1, n)]
    for m in range(0, groups, 2):
        pieces[m + 1] = swap(pieces[m], "aa", 1)
    rows = call(
        functools.partial(top_rows_kernel, n, groups),
        shape((rank, groups * rank)),
        [vmem] * n,
        scratch=[pltpu.VMEM((rank, groups * rank), F32)],
        moved=4 * rank * groups * rank,
    )(*tops)
    corrections = call(
        functools.partial(top_kernel, n, groups),
        [shape((share, rank))] * n,
        [vmem] * (2 + n + groups),
        flops=2 * share * rank * (groups + n) * rank,
        moved=4 * share * n * rank,
    )(rows, level, own, *received, *[pieces[m] for m in range(groups)])
    back = [corrections[0]] + [swap(corrections[k], "ba", k) for k in range(1, n)]
    down = call(
        down_kernel,
        shape((points, rank)),
        [hbm] * 4 + [unread],
        scratch=[like(x) for x in (order, skel, inverse, basis)] + [pltpu.SemaphoreType.DMA((3 + PIECES,))],
        flops=2 * points * points * 3 * rank,
        moved=2 * points * (points + 2 * rank),
    )(order, skel, inverse, basis, corrections[0])
    return call(
        functools.partial(final_kernel, n),
        shape((points, cols)),
        [vmem] * (2 + n),
        out_specs=hbm,
        scratch=[pltpu.VMEM((cols, rank), BF), pltpu.VMEM((points, cols), BF), pltpu.SemaphoreType.DMA((PIECES,))],
        flops=2 * points * cols * rank,
        moved=4 * points * cols,
    )(applied, down, *back)


def solution(mesh):
    spec = P(("aa", "ba"), None)
    return jax.shard_map(
        functools.partial(shards, mesh.shape["ba"], mesh.shape["aa"]),
        mesh=mesh,
        in_specs=(spec,) * 8,
        out_specs=spec,
        check_vma=False,
    )
```

```python
import functools

import jax
import jax.numpy as jnp
from jax import lax
from jax.experimental import pallas as pl
from jax.experimental.pallas import tpu as pltpu
from jax.sharding import PartitionSpec as P

BF = jnp.bfloat16
F32 = jnp.float32
NN = (((1,), (0,)), ((), ()))
NT = (((1,), (1,)), ((), ()))
TN = (((0,), (0,)), ((), ()))


def dot(a, b, dims=NN):
    return lax.dot_general(a, b, dims, preferred_element_type=F32)


def partners(n, k):
    half = (n - 2) // 2
    return [(k - 1 + j) % (n - 1) + 1 for j in range(1, half + 1)]


def column_of(row, count):
    wide = jnp.broadcast_to(row.astype(F32), (count, row.shape[1]))
    return wide.T.astype(jnp.int32)


def order_rows(order, size):
    return jnp.where(
        lax.broadcasted_iota(jnp.int32, (size, size), 0) == order, 1.0, 0.0
    ).astype(BF)


def basis_pair(skel, basis):
    points, rank = basis.shape
    ones = jnp.where(
        lax.broadcasted_iota(jnp.int32, (points, rank), 0) == skel, 1.0, 0.0
    ).astype(BF)
    return jnp.concatenate([basis, ones], axis=1)


def fetch(sources, sems):
    copies = [pltpu.make_async_copy(src, dst, sems.at[j]) for j, (src, dst) in enumerate(sources)]
    for copy in copies:
        copy.start()
    return copies


def pieces_of(ref, count):
    rows = ref.shape[0] // count
    return [ref.at[pl.ds(j * rows, rows)] for j in range(count)]


PIECES = 4


def front_kernel(
    n, order_hbm, skel_hbm, sides_hbm, inverse_hbm, basis_hbm, core_hbm, transfer_hbm, top_hbm, *rest
):
    messages, own_ref = rest[: n - 1], rest[n - 1]
    sides_ref, inverse_ref, placed_ref, pair_ref = rest[n : n + 4]
    order_ref, skel_ref, basis_ref, core_ref, transfer_ref, top_ref, coeffs, sems = rest[n + 4 :]
    me = lax.axis_index("ba")
    points, rank = basis_ref.shape
    rows = points // PIECES
    copies = fetch(
        [(skel_hbm, skel_ref), (basis_hbm, basis_ref), (order_hbm, order_ref)]
        + list(zip(pieces_of(inverse_hbm, PIECES), pieces_of(inverse_ref, PIECES)))
        + [(sides_hbm, sides_ref), (core_hbm, core_ref), (transfer_hbm, transfer_ref), (top_hbm, top_ref)],
        sems,
    )
    share = coeffs.shape[0] // n
    for copy in copies[:3]:
        copy.wait()
    pair_ref[...] = basis_pair(skel_ref[...], basis_ref[...])
    placed_ref[...] = order_rows(order_ref[...], points)
    both = None
    for j in range(PIECES):
        copies[3 + j].wait()
        at = slice(j * rows, (j + 1) * rows)
        part = dot(pair_ref[at, :], inverse_ref[at, :], TN)
        both = part if both is None else both + part
    up = (both[:rank] + both[rank:]).astype(BF)
    up = dot(up, placed_ref[...], NT).astype(BF)
    for copy in copies[3 + PIECES :]:
        copy.wait()
    coeffs[...] = dot(up, sides_ref[...]).T.astype(BF)
    transfer = transfer_ref[...].astype(BF)
    groups = top_ref.shape[1] // rank
    top = top_ref[...].astype(F32)
    top = jnp.concatenate([top[:, g * rank : (g + 1) * rank] for g in range(groups)], axis=0).astype(BF)

    def block(m):
        return core_ref[:, pl.ds(pl.multiple_of((me ^ m) * rank, rank), rank)]

    for k in range(n):
        out = own_ref if k == 0 else messages[k - 1]
        out[0:share, :] = coeffs[pl.ds(pl.multiple_of((me ^ k) * share, share), share), :]
        out[share : share + rank, :] = transfer
        at = share + rank
        for m in range(n) if k == 0 else [0] + [k ^ m for m in partners(n, k)]:
            out[at : at + rank, :] = block(m)
            at += rank
        out[at:, :] = top


def leaf_kernel(order_ref, sides_ref, inverse_ref, placed_ref, pair_ref, applied_ref, down_ref):
    points, cols = sides_ref.shape
    rank = down_ref.shape[1]
    column = column_of(order_ref[...], 128)
    lanes = lax.broadcasted_iota(jnp.int32, (points, 128), 1)
    gather = jnp.concatenate(
        [jnp.where(column == lanes + j * 128, 1.0, 0.0).astype(BF) for j in range(points // 128)], axis=1
    )
    ordered = dot(gather, sides_ref[...]).astype(BF)
    applied = dot(inverse_ref[...], ordered).astype(BF)
    both = dot(inverse_ref[...], pair_ref[...])
    down = (both[:, :rank] + both[:, rank:]).astype(BF)
    applied_ref[...] = dot(placed_ref[...], applied).astype(BF)
    down_ref[...] = dot(placed_ref[...], down).astype(BF)


def group_kernel(n, rank, after, own_ref, *rest):
    del after
    messages, (level_ref, group_ref) = rest[: n - 1], rest[n - 1 :]
    share = level_ref.shape[0]
    core = {}
    for k in range(n):
        at = share + rank
        for m in range(n) if k == 0 else [k] + partners(n, k):
            core[k, m] = own_ref[at : at + rank, :] if k == 0 else messages[k - 1][at : at + rank, :]
            at += rank
    coeffs = [msg[0:share, :] for msg in (own_ref,) + messages]
    transfers = [msg[share : share + rank, :] for msg in (own_ref,) + messages]
    total = None
    for k in range(n):
        level = None
        for m in range(n):
            term = dot(coeffs[m], core[m, k]) if (m, k) in core else dot(coeffs[m], core[k, m], NT)
            level = term if level is None else level + term
        level_ref[:, k * rank : (k + 1) * rank] = level
        rest_of = (coeffs[k].astype(F32) - level).astype(BF)
        term = dot(rest_of, transfers[k])
        total = term if total is None else total + term
    group_ref[...] = total.astype(BF)


def top_rows_kernel(n, groups, *rest):
    messages, (rows_ref, held) = rest[:n], rest[n:]
    me = lax.axis_index("ba")
    mine = lax.axis_index("aa")
    rank = rows_ref.shape[0]
    part = rank // n
    for k in range(n):
        tail = messages[k][messages[k].shape[0] - groups * part :, :].astype(F32)
        for g in range(groups):
            held[pl.ds(pl.multiple_of((me ^ k) * part, part), part), g * rank : (g + 1) * rank] = tail[
                g * part : (g + 1) * part
            ]
    for m in range(groups):
        rows_ref[:, m * rank : (m + 1) * rank] = held[
            :, pl.ds(pl.multiple_of((mine ^ m) * rank, rank), rank)
        ].astype(BF)


def top_kernel(n, groups, rows_ref, level_ref, *rest):
    messages, pieces, outs = rest[:n], rest[n : n + groups], rest[n + groups :]
    share = level_ref.shape[0]
    rank = rows_ref.shape[0]
    stacked = jnp.concatenate([piece[...] for piece in pieces], axis=1)
    top = dot(stacked, rows_ref[...], NT).astype(BF)
    transfers = jnp.concatenate([msg[share : share + rank, :] for msg in messages], axis=0)
    correction = (level_ref[...] + dot(top, transfers, NT)).astype(BF)
    for k in range(n):
        outs[k][...] = correction[:, k * rank : (k + 1) * rank]


def final_kernel(n, applied_ref, down_ref, *rest):
    pieces, (out_hbm, correction, out_ref, sems) = rest[:n], rest[n:]
    me = lax.axis_index("ba")
    share = pieces[0].shape[0]
    for k in range(n):
        correction[pl.ds(pl.multiple_of((me ^ k) * share, share), share), :] = pieces[k][...]
    rows = out_ref.shape[0] // PIECES
    copies = []
    for j, (src, dst) in enumerate(zip(pieces_of(out_ref, PIECES), pieces_of(out_hbm, PIECES))):
        at = slice(j * rows, (j + 1) * rows)
        out_ref[at, :] = (
            applied_ref[at, :].astype(F32) - dot(down_ref[at, :], correction[...], NT)
        ).astype(BF)
        copies.append(pltpu.make_async_copy(src, dst, sems.at[j]))
        copies[-1].start()
    for copy in copies:
        copy.wait()


def shape(dims, kind=BF):
    return jax.ShapeDtypeStruct(dims, kind)


def call(body, outs, in_specs, out_specs=None, scratch=(), flops=0, moved=0, limit=32):
    return pl.pallas_call(
        body,
        out_shape=outs,
        in_specs=in_specs,
        scratch_shapes=list(scratch),
        compiler_params=pltpu.CompilerParams(vmem_limit_bytes=limit * 1024 * 1024),
        cost_estimate=pl.CostEstimate(flops=flops, bytes_accessed=moved, transcendentals=0),
        **({} if out_specs is None else {"out_specs": out_specs}),
    )


def shards(n, groups, sides, order, skel, inverse, basis, core, transfer, top):
    points, cols = sides.shape
    rank = basis.shape[1]
    share = cols // n
    vmem = pl.BlockSpec(memory_space=pltpu.VMEM)
    hbm = pl.BlockSpec(memory_space=pltpu.HBM)
    unread = pl.BlockSpec(memory_space=pl.ANY)

    def far(*arrays):
        return [pltpu.with_memory_space_constraint(x, pltpu.HBM) for x in arrays]

    def like(array):
        return pltpu.VMEM(array.shape, array.dtype)

    def swap(array, axis, k):
        size = {"aa": groups, "ba": n}[axis]
        return lax.ppermute(array, axis, [(i, i ^ k) for i in range(size)])

    tail = rank + groups * top.shape[0]
    sizes = [share + rank * (1 + len(partners(n, k))) + tail for k in range(1, n)] + [share + rank * n + tail]
    *messages, own, sides_held, inverse_held, placed, pair = call(
        functools.partial(front_kernel, n),
        [shape((size, rank)) for size in sizes]
        + [shape(sides.shape), shape(inverse.shape), shape((points, points)), shape((points, 2 * rank))],
        [hbm] * 8,
        scratch=[like(x) for x in (order, skel, basis, core, transfer, top)]
        + [pltpu.VMEM((cols, rank), BF), pltpu.SemaphoreType.DMA((7 + PIECES,))],
        flops=2 * rank * points * (3 * points + cols),
        moved=2 * points * (points + cols + rank),
    )(*far(order, skel, sides, inverse, basis, core, transfer, top))
    received = [swap(messages[k - 1], "ba", k) for k in range(1, n)]
    applied, down = call(
        leaf_kernel,
        [shape((points, cols)), shape((points, rank))],
        [vmem] * 5,
        flops=2 * points * points * 3 * (cols + rank),
        moved=2 * points * (points + 2 * cols),
    )(order, sides_held, inverse_held, placed, pair)
    level, group = call(
        functools.partial(group_kernel, n, rank),
        [shape((share, n * rank), F32), shape((share, rank))],
        [unread] + [vmem] * n,
        flops=2 * share * n * rank * (n + 1) * rank,
        moved=4 * share * n * rank,
    )(down, own, *received)
    pieces = {0: group}
    for m in range(2, groups, 2):
        pieces[m] = swap(group, "aa", m)
    for m in range(0, groups, 2):
        pieces[m + 1] = swap(pieces[m], "aa", 1)
    rows = call(
        functools.partial(top_rows_kernel, n, groups),
        shape((rank, groups * rank)),
        [vmem] * n,
        scratch=[pltpu.VMEM((rank, groups * rank), F32)],
        moved=4 * rank * groups * rank,
    )(own, *received)
    corrections = call(
        functools.partial(top_kernel, n, groups),
        [shape((share, rank))] * n,
        [vmem] * (2 + n + groups),
        flops=2 * share * rank * (groups + n) * rank,
        moved=4 * share * n * rank,
    )(rows, level, own, *received, *[pieces[m] for m in range(groups)])
    back = [corrections[0]] + [swap(corrections[k], "ba", k) for k in range(1, n)]
    return call(
        functools.partial(final_kernel, n),
        shape((points, cols)),
        [vmem] * (2 + n),
        out_specs=hbm,
        scratch=[pltpu.VMEM((cols, rank), BF), pltpu.VMEM((points, cols), BF), pltpu.SemaphoreType.DMA((PIECES,))],
        flops=2 * points * cols * rank,
        moved=4 * points * cols,
    )(applied, down, *back)


def solution(mesh):
    spec = P(("aa", "ba"), None)
    return jax.shard_map(
        functools.partial(shards, mesh.shape["ba"], mesh.shape["aa"]),
        mesh=mesh,
        in_specs=(spec,) * 8,
        out_specs=spec,
        check_vma=False,
    )
```

```python
import functools

import jax
import jax.numpy as jnp
from jax import lax
from jax.experimental import pallas as pl
from jax.experimental.pallas import tpu as pltpu
from jax.sharding import PartitionSpec as P

BF = jnp.bfloat16
F32 = jnp.float32
NN = (((1,), (0,)), ((), ()))
NT = (((1,), (1,)), ((), ()))
TN = (((0,), (0,)), ((), ()))


def dot(a, b, dims=NN):
    return lax.dot_general(a, b, dims, preferred_element_type=F32)


def partners(n, k):
    half = (n - 2) // 2
    return [(k - 1 + j) % (n - 1) + 1 for j in range(1, half + 1)]


def column_of(row, count):
    wide = jnp.broadcast_to(row.astype(F32), (count, row.shape[1]))
    return wide.T.astype(jnp.int32)


def order_rows(order, size):
    return jnp.where(
        lax.broadcasted_iota(jnp.int32, (size, size), 0) == order, 1.0, 0.0
    ).astype(BF)


def order_columns(order, size):
    column = column_of(order, 128)
    lanes = lax.broadcasted_iota(jnp.int32, (size, 128), 1)
    return jnp.concatenate(
        [jnp.where(column == lanes + j * 128, 1.0, 0.0).astype(BF) for j in range(size // 128)], axis=1
    )


def basis_pair(skel, basis):
    points, rank = basis.shape
    ones = jnp.where(
        lax.broadcasted_iota(jnp.int32, (points, rank), 0) == skel, 1.0, 0.0
    ).astype(BF)
    return jnp.concatenate([basis, ones], axis=1)


def fetch(sources, sems):
    copies = [pltpu.make_async_copy(src, dst, sems.at[j]) for j, (src, dst) in enumerate(sources)]
    for copy in copies:
        copy.start()
    return copies


def pieces_of(ref, count):
    rows = ref.shape[0] // count
    return [ref.at[pl.ds(j * rows, rows)] for j in range(count)]


PIECES = 4


def front_kernel(
    n, order_hbm, skel_hbm, sides_hbm, inverse_hbm, basis_hbm, core_hbm, transfer_hbm, top_hbm, *rest
):
    messages, own_ref = rest[: n - 1], rest[n - 1]
    sides_ref, inverse_ref, gather_ref, placed_ref, pair_ref, top_ref = rest[n : n + 6]
    order_ref, skel_ref, basis_ref, core_ref, transfer_ref, coeffs, sems = rest[n + 6 :]
    me = lax.axis_index("ba")
    points, rank = basis_ref.shape
    rows = points // PIECES
    copies = fetch(
        [(skel_hbm, skel_ref), (basis_hbm, basis_ref), (order_hbm, order_ref)]
        + list(zip(pieces_of(inverse_hbm, PIECES), pieces_of(inverse_ref, PIECES)))
        + [(sides_hbm, sides_ref), (core_hbm, core_ref), (transfer_hbm, transfer_ref), (top_hbm, top_ref)],
        sems,
    )
    share = coeffs.shape[0] // n
    for copy in copies[:3]:
        copy.wait()
    pair_ref[...] = basis_pair(skel_ref[...], basis_ref[...])
    gather_ref[...] = order_columns(order_ref[...], points)
    placed_ref[...] = order_rows(order_ref[...], points)
    both = None
    for j in range(PIECES):
        copies[3 + j].wait()
        at = slice(j * rows, (j + 1) * rows)
        part = dot(pair_ref[at, :], inverse_ref[at, :], TN)
        both = part if both is None else both + part
    up = (both[:rank] + both[rank:]).astype(BF)
    up = dot(up, gather_ref[...]).astype(BF)
    for copy in copies[3 + PIECES :]:
        copy.wait()
    coeffs[...] = dot(up, sides_ref[...]).T.astype(BF)
    transfer = transfer_ref[...].astype(BF)

    def block(m):
        return core_ref[:, pl.ds(pl.multiple_of((me ^ m) * rank, rank), rank)]

    for k in range(n):
        out = own_ref if k == 0 else messages[k - 1]
        out[0:share, :] = coeffs[pl.ds(pl.multiple_of((me ^ k) * share, share), share), :]
        out[share : share + rank, :] = transfer
        at = share + rank
        for m in range(n) if k == 0 else [0] + [k ^ m for m in partners(n, k)]:
            out[at : at + rank, :] = block(m)
            at += rank


def applied_kernel(sides_ref, inverse_ref, gather_ref, top_ref, applied_ref, top_out):
    ordered = dot(gather_ref[...], sides_ref[...]).astype(BF)
    applied_ref[...] = dot(inverse_ref[...], ordered).astype(BF)
    top_out[...] = top_ref[...]


def down_kernel(inverse_ref, placed_ref, pair_ref, applied_ref, after, applied_out, down_ref):
    del after
    rank = down_ref.shape[1]
    both = dot(inverse_ref[...], pair_ref[...])
    down = (both[:, :rank] + both[:, rank:]).astype(BF)
    applied_out[...] = dot(placed_ref[...], applied_ref[...]).astype(BF)
    down_ref[...] = dot(placed_ref[...], down).astype(BF)


def group_kernel(n, rank, after, own_ref, *rest):
    del after
    messages, (level_ref, group_ref) = rest[: n - 1], rest[n - 1 :]
    share = level_ref.shape[0]
    core = {}
    for k in range(n):
        at = share + rank
        for m in range(n) if k == 0 else [k] + partners(n, k):
            core[k, m] = own_ref[at : at + rank, :] if k == 0 else messages[k - 1][at : at + rank, :]
            at += rank
    coeffs = [msg[0:share, :] for msg in (own_ref,) + messages]
    transfers = [msg[share : share + rank, :] for msg in (own_ref,) + messages]
    total = None
    for k in range(n):
        level = None
        for m in range(n):
            term = dot(coeffs[m], core[m, k]) if (m, k) in core else dot(coeffs[m], core[k, m], NT)
            level = term if level is None else level + term
        level_ref[:, k * rank : (k + 1) * rank] = level
        rest_of = (coeffs[k].astype(F32) - level).astype(BF)
        term = dot(rest_of, transfers[k])
        total = term if total is None else total + term
    group_ref[...] = total.astype(BF)


def top_rows_kernel(n, groups, *rest):
    tops, (rows_ref, held) = rest[:n], rest[n:]
    me = lax.axis_index("ba")
    mine = lax.axis_index("aa")
    part = tops[0].shape[0]
    rank = rows_ref.shape[0]
    for k in range(n):
        held[pl.ds(pl.multiple_of((me ^ k) * part, part), part), :] = tops[k][...].astype(F32)
    for m in range(groups):
        rows_ref[:, m * rank : (m + 1) * rank] = held[
            :, pl.ds(pl.multiple_of((mine ^ m) * rank, rank), rank)
        ].astype(BF)


def top_kernel(n, groups, rows_ref, level_ref, *rest):
    messages, pieces, outs = rest[:n], rest[n : n + groups], rest[n + groups :]
    share = level_ref.shape[0]
    rank = rows_ref.shape[0]
    stacked = jnp.concatenate([piece[...] for piece in pieces], axis=1)
    top = dot(stacked, rows_ref[...], NT).astype(BF)
    transfers = jnp.concatenate([msg[share : share + rank, :] for msg in messages], axis=0)
    correction = (level_ref[...] + dot(top, transfers, NT)).astype(BF)
    for k in range(n):
        outs[k][...] = correction[:, k * rank : (k + 1) * rank]


def final_kernel(n, applied_ref, down_ref, *rest):
    pieces, (out_hbm, correction, out_ref, sems) = rest[:n], rest[n:]
    me = lax.axis_index("ba")
    share = pieces[0].shape[0]
    for k in range(n):
        correction[pl.ds(pl.multiple_of((me ^ k) * share, share), share), :] = pieces[k][...]
    rows = out_ref.shape[0] // PIECES
    copies = []
    for j, (src, dst) in enumerate(zip(pieces_of(out_ref, PIECES), pieces_of(out_hbm, PIECES))):
        at = slice(j * rows, (j + 1) * rows)
        out_ref[at, :] = (
            applied_ref[at, :].astype(F32) - dot(down_ref[at, :], correction[...], NT)
        ).astype(BF)
        copies.append(pltpu.make_async_copy(src, dst, sems.at[j]))
        copies[-1].start()
    for copy in copies:
        copy.wait()


def shape(dims, kind=BF):
    return jax.ShapeDtypeStruct(dims, kind)


def call(body, outs, in_specs, out_specs=None, scratch=(), flops=0, moved=0, limit=32):
    return pl.pallas_call(
        body,
        out_shape=outs,
        in_specs=in_specs,
        scratch_shapes=list(scratch),
        compiler_params=pltpu.CompilerParams(vmem_limit_bytes=limit * 1024 * 1024),
        cost_estimate=pl.CostEstimate(flops=flops, bytes_accessed=moved, transcendentals=0),
        **({} if out_specs is None else {"out_specs": out_specs}),
    )


def shards(n, groups, sides, order, skel, inverse, basis, core, transfer, top):
    points, cols = sides.shape
    rank = basis.shape[1]
    share = cols // n
    vmem = pl.BlockSpec(memory_space=pltpu.VMEM)
    hbm = pl.BlockSpec(memory_space=pltpu.HBM)
    unread = pl.BlockSpec(memory_space=pl.ANY)

    def far(*arrays):
        return [pltpu.with_memory_space_constraint(x, pltpu.HBM) for x in arrays]

    def like(array):
        return pltpu.VMEM(array.shape, array.dtype)

    def swap(array, axis, k):
        size = {"aa": groups, "ba": n}[axis]
        return lax.ppermute(array, axis, [(i, i ^ k) for i in range(size)])

    sizes = [share + rank * (2 + len(partners(n, k))) for k in range(1, n)] + [share + rank * (n + 1)]
    *messages, own, sides_held, inverse_held, gather, placed, pair, top_held = call(
        functools.partial(front_kernel, n),
        [shape((size, rank)) for size in sizes]
        + [shape(sides.shape), shape(inverse.shape)]
        + [shape((points, points))] * 2
        + [shape((points, 2 * rank)), shape(top.shape)],
        [hbm] * 8,
        scratch=[like(x) for x in (order, skel, basis, core, transfer)]
        + [pltpu.VMEM((cols, rank), BF), pltpu.SemaphoreType.DMA((7 + PIECES,))],
        flops=2 * rank * points * (3 * points + cols),
        moved=2 * points * (points + cols + rank),
    )(*far(order, skel, sides, inverse, basis, core, transfer, top))
    received = [swap(messages[k - 1], "ba", k) for k in range(1, n)]
    applied, top_held = call(
        applied_kernel,
        [shape((points, cols)), shape(top.shape)],
        [vmem] * 4,
        flops=4 * points * points * cols,
        moved=2 * points * (points + 2 * cols),
    )(sides_held, inverse_held, gather, top_held)
    tops = [top_held] + [swap(top_held, "ba", k) for k in range(1, n)]
    level, group = call(
        functools.partial(group_kernel, n, rank),
        [shape((share, n * rank), F32), shape((share, rank))],
        [unread] + [vmem] * n,
        flops=2 * share * n * rank * (n + 1) * rank,
        moved=4 * share * n * rank,
    )(applied, own, *received)
    pieces = {0: group}
    for m in range(2, groups, 2):
        pieces[m] = swap(group, "aa", m)
    for m in range(0, groups, 2):
        pieces[m + 1] = swap(pieces[m], "aa", 1)
    rows = call(
        functools.partial(top_rows_kernel, n, groups),
        shape((rank, groups * rank)),
        [vmem] * n,
        scratch=[pltpu.VMEM((rank, groups * rank), F32)],
        moved=4 * rank * groups * rank,
    )(*tops)
    corrections = call(
        functools.partial(top_kernel, n, groups),
        [shape((share, rank))] * n,
        [vmem] * (2 + n + groups),
        flops=2 * share * rank * (groups + n) * rank,
        moved=4 * share * n * rank,
    )(rows, level, own, *received, *[pieces[m] for m in range(groups)])
    back = [corrections[0]] + [swap(corrections[k], "ba", k) for k in range(1, n)]
    applied, down = call(
        down_kernel,
        [shape((points, cols)), shape((points, rank))],
        [vmem] * 4 + [unread],
        flops=2 * points * points * (3 * rank + cols),
        moved=2 * points * (points + 2 * cols),
    )(inverse_held, placed, pair, applied, corrections[0])
    return call(
        functools.partial(final_kernel, n),
        shape((points, cols)),
        [vmem] * (2 + n),
        out_specs=hbm,
        scratch=[pltpu.VMEM((cols, rank), BF), pltpu.VMEM((points, cols), BF), pltpu.SemaphoreType.DMA((PIECES,))],
        flops=2 * points * cols * rank,
        moved=4 * points * cols,
    )(applied, down, *back)


def solution(mesh):
    spec = P(("aa", "ba"), None)
    return jax.shard_map(
        functools.partial(shards, mesh.shape["ba"], mesh.shape["aa"]),
        mesh=mesh,
        in_specs=(spec,) * 8,
        out_specs=spec,
        check_vma=False,
    )
```

```python
import functools

import jax
import jax.numpy as jnp
from jax import lax
from jax.experimental import pallas as pl
from jax.experimental.pallas import tpu as pltpu
from jax.sharding import PartitionSpec as P

BF = jnp.bfloat16
F32 = jnp.float32
NN = (((1,), (0,)), ((), ()))
NT = (((1,), (1,)), ((), ()))
TN = (((0,), (0,)), ((), ()))


def dot(a, b, dims=NN):
    return lax.dot_general(a, b, dims, preferred_element_type=F32)


def partners(n, k):
    half = (n - 2) // 2
    return [(k - 1 + j) % (n - 1) + 1 for j in range(1, half + 1)]


def column_of(row, count):
    wide = jnp.broadcast_to(row.astype(F32), (count, row.shape[1]))
    return wide.T.astype(jnp.int32)


def order_rows(order, size):
    return jnp.where(
        lax.broadcasted_iota(jnp.int32, (size, size), 0) == order, 1.0, 0.0
    ).astype(BF)


def order_columns(order, size):
    column = column_of(order, 128)
    lanes = lax.broadcasted_iota(jnp.int32, (size, 128), 1)
    return jnp.concatenate(
        [jnp.where(column == lanes + j * 128, 1.0, 0.0).astype(BF) for j in range(size // 128)], axis=1
    )


def basis_pair(skel, basis):
    points, rank = basis.shape
    ones = jnp.where(
        lax.broadcasted_iota(jnp.int32, (points, rank), 0) == skel, 1.0, 0.0
    ).astype(BF)
    return jnp.concatenate([basis, ones], axis=1)


def fetch(sources, sems):
    copies = [pltpu.make_async_copy(src, dst, sems.at[j]) for j, (src, dst) in enumerate(sources)]
    for copy in copies:
        copy.start()
    return copies


def pieces_of(ref, count):
    rows = ref.shape[0] // count
    return [ref.at[pl.ds(j * rows, rows)] for j in range(count)]


PIECES = 4


def front_kernel(
    n, order_hbm, skel_hbm, sides_hbm, inverse_hbm, basis_hbm, core_hbm, transfer_hbm, top_hbm, *rest
):
    messages, own_ref = rest[: n - 1], rest[n - 1]
    sides_ref, inverse_ref, gather_ref, pair_ref, top_ref, order_ref = rest[n : n + 6]
    skel_ref, basis_ref, core_ref, transfer_ref, coeffs, sems = rest[n + 6 :]
    me = lax.axis_index("ba")
    points, rank = basis_ref.shape
    rows = points // PIECES
    copies = fetch(
        [(skel_hbm, skel_ref), (basis_hbm, basis_ref), (order_hbm, order_ref)]
        + list(zip(pieces_of(inverse_hbm, PIECES), pieces_of(inverse_ref, PIECES)))
        + [(sides_hbm, sides_ref), (core_hbm, core_ref), (transfer_hbm, transfer_ref), (top_hbm, top_ref)],
        sems,
    )
    share = coeffs.shape[0] // n
    for copy in copies[:3]:
        copy.wait()
    pair_ref[...] = basis_pair(skel_ref[...], basis_ref[...])
    gather_ref[...] = order_columns(order_ref[...], points)
    both = None
    for j in range(PIECES):
        copies[3 + j].wait()
        at = slice(j * rows, (j + 1) * rows)
        part = dot(pair_ref[at, :], inverse_ref[at, :], TN)
        both = part if both is None else both + part
    up = (both[:rank] + both[rank:]).astype(BF)
    up = dot(up, gather_ref[...]).astype(BF)
    for copy in copies[3 + PIECES :]:
        copy.wait()
    coeffs[...] = dot(up, sides_ref[...]).T.astype(BF)
    transfer = transfer_ref[...].astype(BF)

    def block(m):
        return core_ref[:, pl.ds(pl.multiple_of((me ^ m) * rank, rank), rank)]

    for k in range(n):
        out = own_ref if k == 0 else messages[k - 1]
        out[0:share, :] = coeffs[pl.ds(pl.multiple_of((me ^ k) * share, share), share), :]
        out[share : share + rank, :] = transfer
        at = share + rank
        for m in range(n) if k == 0 else [0] + [k ^ m for m in partners(n, k)]:
            out[at : at + rank, :] = block(m)
            at += rank


def applied_kernel(sides_ref, inverse_ref, gather_ref, top_ref, applied_ref, top_out):
    ordered = dot(gather_ref[...], sides_ref[...]).astype(BF)
    applied_ref[...] = dot(inverse_ref[...], ordered).astype(BF)
    top_out[...] = top_ref[...]


def down_kernel(inverse_ref, order_ref, pair_ref, applied_ref, after, applied_out, down_ref):
    del after
    points, rank = down_ref.shape
    placed = order_rows(order_ref[...], points)
    both = dot(inverse_ref[...], pair_ref[...])
    down = (both[:, :rank] + both[:, rank:]).astype(BF)
    applied_out[...] = dot(placed, applied_ref[...]).astype(BF)
    down_ref[...] = dot(placed, down).astype(BF)


def group_kernel(n, rank, after, own_ref, *rest):
    del after
    messages, (level_ref, group_ref) = rest[: n - 1], rest[n - 1 :]
    share = level_ref.shape[0]
    messages = messages[::-1]
    coeffs = [msg[0:share, :] for msg in (own_ref,) + messages]
    transfers = [msg[share : share + rank, :] for msg in (own_ref,) + messages]
    level = [None] * n

    def add(k, term):
        level[k] = term if level[k] is None else level[k] + term

    for k in range(n):
        msg = own_ref if k == 0 else messages[k - 1]
        which = list(range(n)) if k == 0 else [k] + partners(n, k)
        blocks = [msg[share + rank * (j + 1) : share + rank * (j + 2), :] for j in range(len(which))]
        wide = dot(coeffs[k], jnp.concatenate(blocks, axis=1))
        for j, m in enumerate(which):
            add(m, wide[:, j * rank : (j + 1) * rank])
        if len(which) > 1:
            others = jnp.concatenate([coeffs[m] for m in which[1:]], axis=1)
            add(k, dot(others, jnp.concatenate(blocks[1:], axis=1), NT))
    level_ref[...] = jnp.concatenate(level, axis=1)
    rest_of = [(coeffs[k].astype(F32) - level[k]).astype(BF) for k in range(n)]
    total = dot(jnp.concatenate(rest_of, axis=1), jnp.concatenate(transfers, axis=0))
    group_ref[...] = total.astype(BF)


def top_rows_kernel(n, groups, *rest):
    tops, (rows_ref, held) = rest[:n], rest[n:]
    me = lax.axis_index("ba")
    mine = lax.axis_index("aa")
    part = tops[0].shape[0]
    rank = rows_ref.shape[0]
    for k in range(n):
        held[pl.ds(pl.multiple_of((me ^ k) * part, part), part), :] = tops[k][...].astype(F32)
    for m in range(groups):
        rows_ref[:, m * rank : (m + 1) * rank] = held[
            :, pl.ds(pl.multiple_of((mine ^ m) * rank, rank), rank)
        ].astype(BF)


def top_kernel(n, groups, rows_ref, level_ref, *rest):
    messages, pieces, outs = rest[:n], rest[n : n + groups], rest[n + groups :]
    share = level_ref.shape[0]
    rank = rows_ref.shape[0]
    stacked = jnp.concatenate([piece[...] for piece in pieces], axis=1)
    top = dot(stacked, rows_ref[...], NT).astype(BF)
    transfers = jnp.concatenate([msg[share : share + rank, :] for msg in messages], axis=0)
    correction = (level_ref[...] + dot(top, transfers, NT)).astype(BF)
    for k in range(n):
        outs[k][...] = correction[:, k * rank : (k + 1) * rank]


def final_kernel(n, applied_ref, down_ref, *rest):
    pieces, (out_hbm, correction, out_ref, sems) = rest[:n], rest[n:]
    me = lax.axis_index("ba")
    share = pieces[0].shape[0]
    for k in range(n):
        correction[pl.ds(pl.multiple_of((me ^ k) * share, share), share), :] = pieces[k][...]
    rows = out_ref.shape[0] // PIECES
    copies = []
    for j, (src, dst) in enumerate(zip(pieces_of(out_ref, PIECES), pieces_of(out_hbm, PIECES))):
        at = slice(j * rows, (j + 1) * rows)
        out_ref[at, :] = (
            applied_ref[at, :].astype(F32) - dot(down_ref[at, :], correction[...], NT)
        ).astype(BF)
        copies.append(pltpu.make_async_copy(src, dst, sems.at[j]))
        copies[-1].start()
    for copy in copies:
        copy.wait()


def shape(dims, kind=BF):
    return jax.ShapeDtypeStruct(dims, kind)


def call(body, outs, in_specs, out_specs=None, scratch=(), flops=0, moved=0, limit=32):
    return pl.pallas_call(
        body,
        out_shape=outs,
        in_specs=in_specs,
        scratch_shapes=list(scratch),
        compiler_params=pltpu.CompilerParams(vmem_limit_bytes=limit * 1024 * 1024),
        cost_estimate=pl.CostEstimate(flops=flops, bytes_accessed=moved, transcendentals=0),
        **({} if out_specs is None else {"out_specs": out_specs}),
    )


def shards(n, groups, sides, order, skel, inverse, basis, core, transfer, top):
    points, cols = sides.shape
    rank = basis.shape[1]
    share = cols // n
    vmem = pl.BlockSpec(memory_space=pltpu.VMEM)
    hbm = pl.BlockSpec(memory_space=pltpu.HBM)
    unread = pl.BlockSpec(memory_space=pl.ANY)

    def far(*arrays):
        return [pltpu.with_memory_space_constraint(x, pltpu.HBM) for x in arrays]

    def like(array):
        return pltpu.VMEM(array.shape, array.dtype)

    def swap(array, axis, k):
        size = {"aa": groups, "ba": n}[axis]
        return lax.ppermute(array, axis, [(i, i ^ k) for i in range(size)])

    sizes = [share + rank * (2 + len(partners(n, k))) for k in range(1, n)] + [share + rank * (n + 1)]
    *messages, own, sides_held, inverse_held, gather, pair, top_held, order_held = call(
        functools.partial(front_kernel, n),
        [shape((size, rank)) for size in sizes]
        + [shape(sides.shape), shape(inverse.shape)]
        + [shape((points, points)), shape((points, 2 * rank)), shape(top.shape), shape(order.shape, order.dtype)],
        [hbm] * 8,
        scratch=[like(x) for x in (skel, basis, core, transfer)]
        + [pltpu.VMEM((cols, rank), BF), pltpu.SemaphoreType.DMA((7 + PIECES,))],
        flops=2 * rank * points * (3 * points + cols),
        moved=2 * points * (points + cols + rank),
    )(*far(order, skel, sides, inverse, basis, core, transfer, top))
    received = [swap(messages[k - 1], "ba", k) for k in range(1, n)]
    applied, top_held = call(
        applied_kernel,
        [shape((points, cols)), shape(top.shape)],
        [vmem] * 4,
        flops=4 * points * points * cols,
        moved=2 * points * (points + 2 * cols),
    )(sides_held, inverse_held, gather, top_held)
    tops = [top_held] + [swap(top_held, "ba", k) for k in range(1, n)]
    level, group = call(
        functools.partial(group_kernel, n, rank),
        [shape((share, n * rank), F32), shape((share, rank))],
        [unread] + [vmem] * n,
        flops=2 * share * n * rank * (n + 1) * rank,
        moved=4 * share * n * rank,
    )(applied, own, *received[::-1])
    pieces = {0: group}
    for m in range(2, groups, 2):
        pieces[m] = swap(group, "aa", m)
    for m in range(0, groups, 2):
        pieces[m + 1] = swap(pieces[m], "aa", 1)
    rows = call(
        functools.partial(top_rows_kernel, n, groups),
        shape((rank, groups * rank)),
        [vmem] * n,
        scratch=[pltpu.VMEM((rank, groups * rank), F32)],
        moved=4 * rank * groups * rank,
    )(*tops)
    corrections = call(
        functools.partial(top_kernel, n, groups),
        [shape((share, rank))] * n,
        [vmem] * (2 + n + groups),
        flops=2 * share * rank * (groups + n) * rank,
        moved=4 * share * n * rank,
    )(rows, level, own, *received, *[pieces[m] for m in range(groups)])
    back = [corrections[0]] + [swap(corrections[k], "ba", k) for k in range(1, n)]
    applied, down = call(
        down_kernel,
        [shape((points, cols)), shape((points, rank))],
        [vmem] * 4 + [unread],
        flops=2 * points * points * (3 * rank + cols),
        moved=2 * points * (points + 2 * cols),
    )(inverse_held, order_held, pair, applied, corrections[0])
    return call(
        functools.partial(final_kernel, n),
        shape((points, cols)),
        [vmem] * (2 + n),
        out_specs=hbm,
        scratch=[pltpu.VMEM((cols, rank), BF), pltpu.VMEM((points, cols), BF), pltpu.SemaphoreType.DMA((PIECES,))],
        flops=2 * points * cols * rank,
        moved=4 * points * cols,
    )(applied, down, *back)


def solution(mesh):
    spec = P(("aa", "ba"), None)
    return jax.shard_map(
        functools.partial(shards, mesh.shape["ba"], mesh.shape["aa"]),
        mesh=mesh,
        in_specs=(spec,) * 8,
        out_specs=spec,
        check_vma=False,
    )
```

```python
import functools

import jax
import jax.numpy as jnp
from jax import lax
from jax.experimental import pallas as pl
from jax.experimental.pallas import tpu as pltpu
from jax.sharding import PartitionSpec as P

BF = jnp.bfloat16
F32 = jnp.float32
NN = (((1,), (0,)), ((), ()))
NT = (((1,), (1,)), ((), ()))
TN = (((0,), (0,)), ((), ()))


def dot(a, b, dims=NN):
    return lax.dot_general(a, b, dims, preferred_element_type=F32)


def partners(n, k):
    half = (n - 2) // 2
    return [(k - 1 + j) % (n - 1) + 1 for j in range(1, half + 1)]


def column_of(row, count):
    wide = jnp.broadcast_to(row.astype(F32), (count, row.shape[1]))
    return wide.T.astype(jnp.int32)


def order_rows(order, size):
    return jnp.where(
        lax.broadcasted_iota(jnp.int32, (size, size), 0) == order, 1.0, 0.0
    ).astype(BF)


def order_columns(order, size):
    column = column_of(order, 128)
    lanes = lax.broadcasted_iota(jnp.int32, (size, 128), 1)
    return jnp.concatenate(
        [jnp.where(column == lanes + j * 128, 1.0, 0.0).astype(BF) for j in range(size // 128)], axis=1
    )


def basis_pair(skel, basis):
    points, rank = basis.shape
    ones = jnp.where(
        lax.broadcasted_iota(jnp.int32, (points, rank), 0) == skel, 1.0, 0.0
    ).astype(BF)
    return jnp.concatenate([basis, ones], axis=1)


def fetch(sources, sems):
    copies = [pltpu.make_async_copy(src, dst, sems.at[j]) for j, (src, dst) in enumerate(sources)]
    for copy in copies:
        copy.start()
    return copies


def pieces_of(ref, count):
    rows = ref.shape[0] // count
    return [ref.at[pl.ds(j * rows, rows)] for j in range(count)]


PIECES = 4


def front_kernel(
    n, order_hbm, skel_hbm, sides_hbm, inverse_hbm, basis_hbm, core_hbm, transfer_hbm, top_hbm, *rest
):
    messages, own_ref = rest[: n - 1], rest[n - 1]
    sides_ref, inverse_ref, gather_ref, pair_ref, top_ref, order_ref = rest[n : n + 6]
    skel_ref, basis_ref, core_ref, transfer_ref, coeffs, sems = rest[n + 6 :]
    me = lax.axis_index("ba")
    points, rank = basis_ref.shape
    rows = points // PIECES
    copies = fetch(
        [(skel_hbm, skel_ref), (basis_hbm, basis_ref), (order_hbm, order_ref)]
        + list(zip(pieces_of(inverse_hbm, PIECES), pieces_of(inverse_ref, PIECES)))
        + [(sides_hbm, sides_ref), (core_hbm, core_ref), (transfer_hbm, transfer_ref), (top_hbm, top_ref)],
        sems,
    )
    share = coeffs.shape[0] // n
    for copy in copies[:3]:
        copy.wait()
    pair_ref[...] = basis_pair(skel_ref[...], basis_ref[...])
    gather_ref[...] = order_columns(order_ref[...], points)
    both = None
    for j in range(PIECES):
        copies[3 + j].wait()
        at = slice(j * rows, (j + 1) * rows)
        part = dot(pair_ref[at, :], inverse_ref[at, :], TN)
        both = part if both is None else both + part
    up = (both[:rank] + both[rank:]).astype(BF)
    up = dot(up, gather_ref[...]).astype(BF)
    for copy in copies[3 + PIECES :]:
        copy.wait()
    coeffs[...] = dot(up, sides_ref[...]).T.astype(BF)
    transfer = transfer_ref[...].astype(BF)

    def block(m):
        return core_ref[:, pl.ds(pl.multiple_of((me ^ m) * rank, rank), rank)]

    for k in range(n):
        out = own_ref if k == 0 else messages[k - 1]
        out[0:share, :] = coeffs[pl.ds(pl.multiple_of((me ^ k) * share, share), share), :]
        out[share : share + rank, :] = transfer
        at = share + rank
        for m in range(n) if k == 0 else [0] + [k ^ m for m in partners(n, k)]:
            out[at : at + rank, :] = block(m)
            at += rank


def ordered_kernel(sides_ref, gather_ref, top_ref, ordered_ref, top_out):
    ordered_ref[...] = dot(gather_ref[...], sides_ref[...]).astype(BF)
    top_out[...] = top_ref[...]


def applied_kernel(inverse_ref, ordered_ref, group_ref, applied_ref, group_out):
    applied_ref[...] = dot(inverse_ref[...], ordered_ref[...]).astype(BF)
    group_out[...] = group_ref[...]


def down_kernel(inverse_ref, order_ref, pair_ref, applied_ref, after, applied_out, down_ref):
    del after
    points, rank = down_ref.shape
    placed = order_rows(order_ref[...], points)
    both = dot(inverse_ref[...], pair_ref[...])
    down = (both[:, :rank] + both[:, rank:]).astype(BF)
    applied_out[...] = dot(placed, applied_ref[...]).astype(BF)
    down_ref[...] = dot(placed, down).astype(BF)


def group_kernel(n, rank, after, own_ref, *rest):
    del after
    messages, (level_ref, group_ref) = rest[: n - 1], rest[n - 1 :]
    share = level_ref.shape[0]
    messages = messages[::-1]
    coeffs = [msg[0:share, :] for msg in (own_ref,) + messages]
    transfers = [msg[share : share + rank, :] for msg in (own_ref,) + messages]
    level = [None] * n

    def add(k, term):
        level[k] = term if level[k] is None else level[k] + term

    for k in range(n):
        msg = own_ref if k == 0 else messages[k - 1]
        which = list(range(n)) if k == 0 else [k] + partners(n, k)
        blocks = [msg[share + rank * (j + 1) : share + rank * (j + 2), :] for j in range(len(which))]
        wide = dot(coeffs[k], jnp.concatenate(blocks, axis=1))
        for j, m in enumerate(which):
            add(m, wide[:, j * rank : (j + 1) * rank])
        if len(which) > 1:
            others = jnp.concatenate([coeffs[m] for m in which[1:]], axis=1)
            add(k, dot(others, jnp.concatenate(blocks[1:], axis=1), NT))
    level_ref[...] = jnp.concatenate(level, axis=1)
    rest_of = [(coeffs[k].astype(F32) - level[k]).astype(BF) for k in range(n)]
    total = dot(jnp.concatenate(rest_of, axis=1), jnp.concatenate(transfers, axis=0))
    group_ref[...] = total.astype(BF)


def top_rows_kernel(n, groups, *rest):
    tops, (rows_ref, held) = rest[:n], rest[n:]
    me = lax.axis_index("ba")
    mine = lax.axis_index("aa")
    part = tops[0].shape[0]
    rank = rows_ref.shape[0]
    for k in range(n):
        held[pl.ds(pl.multiple_of((me ^ k) * part, part), part), :] = tops[k][...].astype(F32)
    for m in range(groups):
        rows_ref[:, m * rank : (m + 1) * rank] = held[
            :, pl.ds(pl.multiple_of((mine ^ m) * rank, rank), rank)
        ].astype(BF)


def top_kernel(n, groups, rows_ref, level_ref, *rest):
    messages, pieces, outs = rest[:n], rest[n : n + groups], rest[n + groups :]
    share = level_ref.shape[0]
    rank = rows_ref.shape[0]
    stacked = jnp.concatenate([piece[...] for piece in pieces], axis=1)
    top = dot(stacked, rows_ref[...], NT).astype(BF)
    transfers = jnp.concatenate([msg[share : share + rank, :] for msg in messages], axis=0)
    correction = (level_ref[...] + dot(top, transfers, NT)).astype(BF)
    for k in range(n):
        outs[k][...] = correction[:, k * rank : (k + 1) * rank]


def final_kernel(n, applied_ref, down_ref, *rest):
    pieces, (out_hbm, correction, out_ref, sems) = rest[:n], rest[n:]
    me = lax.axis_index("ba")
    share = pieces[0].shape[0]
    for k in range(n):
        correction[pl.ds(pl.multiple_of((me ^ k) * share, share), share), :] = pieces[k][...]
    rows = out_ref.shape[0] // PIECES
    copies = []
    for j, (src, dst) in enumerate(zip(pieces_of(out_ref, PIECES), pieces_of(out_hbm, PIECES))):
        at = slice(j * rows, (j + 1) * rows)
        out_ref[at, :] = (
            applied_ref[at, :].astype(F32) - dot(down_ref[at, :], correction[...], NT)
        ).astype(BF)
        copies.append(pltpu.make_async_copy(src, dst, sems.at[j]))
        copies[-1].start()
    for copy in copies:
        copy.wait()


def shape(dims, kind=BF):
    return jax.ShapeDtypeStruct(dims, kind)


def call(body, outs, in_specs, out_specs=None, scratch=(), flops=0, moved=0, limit=32):
    return pl.pallas_call(
        body,
        out_shape=outs,
        in_specs=in_specs,
        scratch_shapes=list(scratch),
        compiler_params=pltpu.CompilerParams(vmem_limit_bytes=limit * 1024 * 1024),
        cost_estimate=pl.CostEstimate(flops=flops, bytes_accessed=moved, transcendentals=0),
        **({} if out_specs is None else {"out_specs": out_specs}),
    )


def shards(n, groups, sides, order, skel, inverse, basis, core, transfer, top):
    points, cols = sides.shape
    rank = basis.shape[1]
    share = cols // n
    vmem = pl.BlockSpec(memory_space=pltpu.VMEM)
    hbm = pl.BlockSpec(memory_space=pltpu.HBM)
    unread = pl.BlockSpec(memory_space=pl.ANY)

    def far(*arrays):
        return [pltpu.with_memory_space_constraint(x, pltpu.HBM) for x in arrays]

    def like(array):
        return pltpu.VMEM(array.shape, array.dtype)

    def swap(array, axis, k):
        size = {"aa": groups, "ba": n}[axis]
        return lax.ppermute(array, axis, [(i, i ^ k) for i in range(size)])

    sizes = [share + rank * (2 + len(partners(n, k))) for k in range(1, n)] + [share + rank * (n + 1)]
    *messages, own, sides_held, inverse_held, gather, pair, top_held, order_held = call(
        functools.partial(front_kernel, n),
        [shape((size, rank)) for size in sizes]
        + [shape(sides.shape), shape(inverse.shape)]
        + [shape((points, points)), shape((points, 2 * rank)), shape(top.shape), shape(order.shape, order.dtype)],
        [hbm] * 8,
        scratch=[like(x) for x in (skel, basis, core, transfer)]
        + [pltpu.VMEM((cols, rank), BF), pltpu.SemaphoreType.DMA((7 + PIECES,))],
        flops=2 * rank * points * (3 * points + cols),
        moved=2 * points * (points + cols + rank),
    )(*far(order, skel, sides, inverse, basis, core, transfer, top))
    received = [swap(messages[k - 1], "ba", k) for k in range(1, n)]
    ordered, top_held = call(
        ordered_kernel,
        [shape((points, cols)), shape(top.shape)],
        [vmem] * 3,
        flops=2 * points * points * cols,
        moved=2 * points * (points + 2 * cols),
    )(sides_held, gather, top_held)
    tops = [top_held] + [swap(top_held, "ba", k) for k in range(1, n)]
    level, group = call(
        functools.partial(group_kernel, n, rank),
        [shape((share, n * rank), F32), shape((share, rank))],
        [unread] + [vmem] * n,
        flops=2 * share * n * rank * (n + 1) * rank,
        moved=4 * share * n * rank,
    )(ordered, own, *received[::-1])
    applied, group_held = call(
        applied_kernel,
        [shape((points, cols)), shape((share, rank))],
        [vmem] * 3,
        flops=2 * points * points * cols,
        moved=2 * points * (points + 2 * cols),
    )(inverse_held, ordered, group)
    pieces = {0: group}
    for m in range(2, groups, 2):
        pieces[m] = swap(group, "aa", m)
    for m in range(0, groups, 2):
        pieces[m + 1] = swap(pieces[m] if m else group_held, "aa", 1)
    rows = call(
        functools.partial(top_rows_kernel, n, groups),
        shape((rank, groups * rank)),
        [vmem] * n,
        scratch=[pltpu.VMEM((rank, groups * rank), F32)],
        moved=4 * rank * groups * rank,
    )(*tops)
    corrections = call(
        functools.partial(top_kernel, n, groups),
        [shape((share, rank))] * n,
        [vmem] * (2 + n + groups),
        flops=2 * share * rank * (groups + n) * rank,
        moved=4 * share * n * rank,
    )(rows, level, own, *received, *[pieces[m] for m in range(groups)])
    back = [corrections[0]] + [swap(corrections[k], "ba", k) for k in range(1, n)]
    applied, down = call(
        down_kernel,
        [shape((points, cols)), shape((points, rank))],
        [vmem] * 4 + [unread],
        flops=2 * points * points * (3 * rank + cols),
        moved=2 * points * (points + 2 * cols),
    )(inverse_held, order_held, pair, applied, corrections[0])
    return call(
        functools.partial(final_kernel, n),
        shape((points, cols)),
        [vmem] * (2 + n),
        out_specs=hbm,
        scratch=[pltpu.VMEM((cols, rank), BF), pltpu.VMEM((points, cols), BF), pltpu.SemaphoreType.DMA((PIECES,))],
        flops=2 * points * cols * rank,
        moved=4 * points * cols,
    )(applied, down, *back)


def solution(mesh):
    spec = P(("aa", "ba"), None)
    return jax.shard_map(
        functools.partial(shards, mesh.shape["ba"], mesh.shape["aa"]),
        mesh=mesh,
        in_specs=(spec,) * 8,
        out_specs=spec,
        check_vma=False,
    )
```

```python
import functools

import jax
import jax.numpy as jnp
from jax import lax
from jax.experimental import pallas as pl
from jax.experimental.pallas import tpu as pltpu
from jax.sharding import PartitionSpec as P

BF = jnp.bfloat16
F32 = jnp.float32
NN = (((1,), (0,)), ((), ()))
NT = (((1,), (1,)), ((), ()))
TN = (((0,), (0,)), ((), ()))


def dot(a, b, dims=NN):
    return lax.dot_general(a, b, dims, preferred_element_type=F32)


def partners(n, k):
    half = (n - 2) // 2
    return [(k - 1 + j) % (n - 1) + 1 for j in range(1, half + 1)]


def column_of(row, count):
    wide = jnp.broadcast_to(row.astype(F32), (count, row.shape[1]))
    return wide.T.astype(jnp.int32)


def order_rows(order, size):
    return jnp.where(
        lax.broadcasted_iota(jnp.int32, (size, size), 0) == order, 1.0, 0.0
    ).astype(BF)


def order_columns(order, size):
    column = column_of(order, 128)
    lanes = lax.broadcasted_iota(jnp.int32, (size, 128), 1)
    return jnp.concatenate(
        [jnp.where(column == lanes + j * 128, 1.0, 0.0).astype(BF) for j in range(size // 128)], axis=1
    )


def basis_pair(skel, basis):
    points, rank = basis.shape
    ones = jnp.where(
        lax.broadcasted_iota(jnp.int32, (points, rank), 0) == skel, 1.0, 0.0
    ).astype(BF)
    return jnp.concatenate([basis, ones], axis=1)


def fetch(sources, sems):
    copies = [pltpu.make_async_copy(src, dst, sems.at[j]) for j, (src, dst) in enumerate(sources)]
    for copy in copies:
        copy.start()
    return copies


def pieces_of(ref, count):
    rows = ref.shape[0] // count
    return [ref.at[pl.ds(j * rows, rows)] for j in range(count)]


PIECES = 4


def pack_kernel(n, core_hbm, transfer_hbm, top_hbm, *rest):
    messages, own_ref = rest[: n - 1], rest[n - 1]
    core_ref, transfer_ref, top_ref, sems = rest[n:]
    me = lax.axis_index("ba")
    rank = transfer_ref.shape[0]
    for copy in fetch([(core_hbm, core_ref), (transfer_hbm, transfer_ref), (top_hbm, top_ref)], sems):
        copy.wait()
    transfer = transfer_ref[...].astype(BF)
    groups = top_ref.shape[1] // rank
    top = top_ref[...].astype(F32)
    top = jnp.concatenate([top[:, g * rank : (g + 1) * rank] for g in range(groups)], axis=0).astype(BF)
    for k in range(n):
        out = own_ref if k == 0 else messages[k - 1]
        out[0:rank, :] = transfer
        at = rank
        for m in range(n) if k == 0 else [0] + [k ^ m for m in partners(n, k)]:
            out[at : at + rank, :] = core_ref[:, pl.ds(pl.multiple_of((me ^ m) * rank, rank), rank)]
            at += rank
        out[at:, :] = top


def front_kernel(n, order_ref, skel_ref, sides_ref, inverse_ref, basis_ref, after, *rest):
    del after
    outs, (gather_ref, pair_ref, coeffs) = rest[:n], rest[n:]
    me = lax.axis_index("ba")
    points, rank = basis_ref.shape
    share = outs[0].shape[0]
    pair = basis_pair(skel_ref[...], basis_ref[...])
    both = dot(pair, inverse_ref[...], TN)
    gather = order_columns(order_ref[...], points)
    up = (both[:rank] + both[rank:]).astype(BF)
    up = dot(up, gather).astype(BF)
    coeffs[...] = dot(up, sides_ref[...]).T.astype(BF)
    for k in range(n):
        outs[k][...] = coeffs[pl.ds(pl.multiple_of((me ^ k) * share, share), share), :]
    gather_ref[...] = gather
    pair_ref[...] = pair


def ordered_kernel(sides_ref, gather_ref, ordered_ref):
    ordered_ref[...] = dot(gather_ref[...], sides_ref[...]).astype(BF)


def applied_kernel(inverse_ref, ordered_ref, group_ref, applied_ref, group_out):
    applied_ref[...] = dot(inverse_ref[...], ordered_ref[...]).astype(BF)
    group_out[...] = group_ref[...]


def down_kernel(inverse_ref, order_ref, pair_ref, applied_ref, after, applied_out, down_ref):
    del after
    points, rank = down_ref.shape
    placed = order_rows(order_ref[...], points)
    both = dot(inverse_ref[...], pair_ref[...])
    down = (both[:, :rank] + both[:, rank:]).astype(BF)
    applied_out[...] = dot(placed, applied_ref[...]).astype(BF)
    down_ref[...] = dot(placed, down).astype(BF)


def group_kernel(n, rank, after, *rest):
    del after
    pieces, messages, (level_ref, group_ref) = rest[:n][::-1], rest[n : 2 * n][::-1], rest[2 * n :]
    coeffs = [piece[...] for piece in pieces]
    transfers = [msg[0:rank, :] for msg in messages]
    level = [None] * n

    def add(k, term):
        level[k] = term if level[k] is None else level[k] + term

    for k in range(n):
        which = list(range(n)) if k == 0 else [k] + partners(n, k)
        blocks = [messages[k][rank * (j + 1) : rank * (j + 2), :] for j in range(len(which))]
        wide = dot(coeffs[k], jnp.concatenate(blocks, axis=1))
        for j, m in enumerate(which):
            add(m, wide[:, j * rank : (j + 1) * rank])
        if len(which) > 1:
            others = jnp.concatenate([coeffs[m] for m in which[1:]], axis=1)
            add(k, dot(others, jnp.concatenate(blocks[1:], axis=1), NT))
    level_ref[...] = jnp.concatenate(level, axis=1)
    rest_of = [(coeffs[k].astype(F32) - level[k]).astype(BF) for k in range(n)]
    total = dot(jnp.concatenate(rest_of, axis=1), jnp.concatenate(transfers, axis=0))
    group_ref[...] = total.astype(BF)


def top_rows_kernel(n, groups, *rest):
    messages, (rows_ref, held) = rest[:n], rest[n:]
    me = lax.axis_index("ba")
    mine = lax.axis_index("aa")
    rank = rows_ref.shape[0]
    part = rank // n
    for k in range(n):
        tail = messages[k][messages[k].shape[0] - groups * part :, :].astype(F32)
        for g in range(groups):
            held[pl.ds(pl.multiple_of((me ^ k) * part, part), part), g * rank : (g + 1) * rank] = tail[
                g * part : (g + 1) * part
            ]
    for m in range(groups):
        rows_ref[:, m * rank : (m + 1) * rank] = held[
            :, pl.ds(pl.multiple_of((mine ^ m) * rank, rank), rank)
        ].astype(BF)


def top_kernel(n, groups, rows_ref, level_ref, *rest):
    messages, pieces, outs = rest[:n], rest[n : n + groups], rest[n + groups :]
    rank = rows_ref.shape[0]
    stacked = jnp.concatenate([piece[...] for piece in pieces], axis=1)
    top = dot(stacked, rows_ref[...], NT).astype(BF)
    transfers = jnp.concatenate([msg[0:rank, :] for msg in messages], axis=0)
    correction = (level_ref[...] + dot(top, transfers, NT)).astype(BF)
    for k in range(n):
        outs[k][...] = correction[:, k * rank : (k + 1) * rank]


def final_kernel(n, applied_ref, down_ref, *rest):
    pieces, (out_hbm, correction, out_ref, sems) = rest[:n], rest[n:]
    me = lax.axis_index("ba")
    share = pieces[0].shape[0]
    for k in range(n):
        correction[pl.ds(pl.multiple_of((me ^ k) * share, share), share), :] = pieces[k][...]
    rows = out_ref.shape[0] // PIECES
    copies = []
    for j, (src, dst) in enumerate(zip(pieces_of(out_ref, PIECES), pieces_of(out_hbm, PIECES))):
        at = slice(j * rows, (j + 1) * rows)
        out_ref[at, :] = (
            applied_ref[at, :].astype(F32) - dot(down_ref[at, :], correction[...], NT)
        ).astype(BF)
        copies.append(pltpu.make_async_copy(src, dst, sems.at[j]))
        copies[-1].start()
    for copy in copies:
        copy.wait()


def shape(dims, kind=BF):
    return jax.ShapeDtypeStruct(dims, kind)


def call(body, outs, in_specs, out_specs=None, scratch=(), flops=0, moved=0, limit=32):
    return pl.pallas_call(
        body,
        out_shape=outs,
        in_specs=in_specs,
        scratch_shapes=list(scratch),
        compiler_params=pltpu.CompilerParams(vmem_limit_bytes=limit * 1024 * 1024),
        cost_estimate=pl.CostEstimate(flops=flops, bytes_accessed=moved, transcendentals=0),
        **({} if out_specs is None else {"out_specs": out_specs}),
    )


def shards(n, groups, sides, order, skel, inverse, basis, core, transfer, top):
    points, cols = sides.shape
    rank = basis.shape[1]
    share = cols // n
    vmem = pl.BlockSpec(memory_space=pltpu.VMEM)
    hbm = pl.BlockSpec(memory_space=pltpu.HBM)
    unread = pl.BlockSpec(memory_space=pl.ANY)

    def far(*arrays):
        return [pltpu.with_memory_space_constraint(x, pltpu.HBM) for x in arrays]

    def like(array):
        return pltpu.VMEM(array.shape, array.dtype)

    def swap(array, axis, k):
        size = {"aa": groups, "ba": n}[axis]
        return lax.ppermute(array, axis, [(i, i ^ k) for i in range(size)])

    tail = groups * top.shape[0]
    sizes = [rank * (2 + len(partners(n, k))) + tail for k in range(1, n)] + [rank * (n + 1) + tail]
    *messages, own = call(
        functools.partial(pack_kernel, n),
        [shape((size, rank)) for size in sizes],
        [hbm] * 3,
        scratch=[like(x) for x in (core, transfer, top)] + [pltpu.SemaphoreType.DMA((3,))],
        flops=16 * points * points * points,
        moved=16 * points * (points + cols + rank),
    )(*far(core, transfer, top))
    received = [own] + [swap(messages[k - 1], "ba", k) for k in range(1, n)]
    *coeffs, gather, pair = call(
        functools.partial(front_kernel, n),
        [shape((share, rank))] * n + [shape((points, points)), shape((points, 2 * rank))],
        [vmem] * 5 + [unread],
        scratch=[pltpu.VMEM((cols, rank), BF)],
        flops=2 * rank * points * (3 * points + cols),
        moved=2 * points * (points + cols + rank),
    )(order, skel, sides, inverse, basis, own)
    coeffs = [coeffs[0]] + [swap(coeffs[k], "ba", k) for k in range(1, n)]
    ordered = call(
        ordered_kernel,
        shape((points, cols)),
        [vmem] * 2,
        flops=2 * points * points * cols,
        moved=2 * points * (points + 2 * cols),
    )(sides, gather)
    rows = call(
        functools.partial(top_rows_kernel, n, groups),
        shape((rank, groups * rank)),
        [vmem] * n,
        scratch=[pltpu.VMEM((rank, groups * rank), F32)],
        moved=4 * rank * groups * rank,
    )(*received)
    level, group = call(
        functools.partial(group_kernel, n, rank),
        [shape((share, n * rank), F32), shape((share, rank))],
        [unread] + [vmem] * (2 * n),
        flops=2 * share * n * rank * (n + 1) * rank,
        moved=4 * share * n * rank,
    )(ordered, *coeffs[::-1], *received[::-1])
    applied, group_held = call(
        applied_kernel,
        [shape((points, cols)), shape((share, rank))],
        [vmem] * 3,
        flops=2 * points * points * cols,
        moved=2 * points * (points + 2 * cols),
    )(inverse, ordered, group)
    pieces = {0: group}
    for m in range(2, groups, 2):
        pieces[m] = swap(group, "aa", m)
    for m in range(0, groups, 2):
        pieces[m + 1] = swap(pieces[m] if m else group_held, "aa", 1)
    corrections = call(
        functools.partial(top_kernel, n, groups),
        [shape((share, rank))] * n,
        [vmem] * (2 + n + groups),
        flops=2 * share * rank * (groups + n) * rank,
        moved=4 * share * n * rank,
    )(rows, level, *received, *[pieces[m] for m in range(groups)])
    back = [corrections[0]] + [swap(corrections[k], "ba", k) for k in range(1, n)]
    applied, down = call(
        down_kernel,
        [shape((points, cols)), shape((points, rank))],
        [vmem] * 4 + [unread],
        flops=2 * points * points * (3 * rank + cols),
        moved=2 * points * (points + 2 * cols),
    )(inverse, order, pair, applied, corrections[0])
    return call(
        functools.partial(final_kernel, n),
        shape((points, cols)),
        [vmem] * (2 + n),
        out_specs=hbm,
        scratch=[pltpu.VMEM((cols, rank), BF), pltpu.VMEM((points, cols), BF), pltpu.SemaphoreType.DMA((PIECES,))],
        flops=2 * points * cols * rank,
        moved=4 * points * cols,
    )(applied, down, *back)


def solution(mesh):
    spec = P(("aa", "ba"), None)
    return jax.shard_map(
        functools.partial(shards, mesh.shape["ba"], mesh.shape["aa"]),
        mesh=mesh,
        in_specs=(spec,) * 8,
        out_specs=spec,
        check_vma=False,
    )
```

```python
import functools

import jax
import jax.numpy as jnp
from jax import lax
from jax.experimental import pallas as pl
from jax.experimental.pallas import tpu as pltpu
from jax.sharding import PartitionSpec as P

BF = jnp.bfloat16
F32 = jnp.float32
NN = (((1,), (0,)), ((), ()))
NT = (((1,), (1,)), ((), ()))
TN = (((0,), (0,)), ((), ()))


def dot(a, b, dims=NN):
    return lax.dot_general(a, b, dims, preferred_element_type=F32)


def partners(n, k):
    half = (n - 2) // 2
    return [(k - 1 + j) % (n - 1) + 1 for j in range(1, half + 1)]


def column_of(row, count):
    wide = jnp.broadcast_to(row.astype(F32), (count, row.shape[1]))
    return wide.T.astype(jnp.int32)


def order_rows(order, size):
    return jnp.where(
        lax.broadcasted_iota(jnp.int32, (size, size), 0) == order, 1.0, 0.0
    ).astype(BF)


def order_columns(order, size):
    column = column_of(order, 128)
    lanes = lax.broadcasted_iota(jnp.int32, (size, 128), 1)
    return jnp.concatenate(
        [jnp.where(column == lanes + j * 128, 1.0, 0.0).astype(BF) for j in range(size // 128)], axis=1
    )


def basis_pair(skel, basis):
    points, rank = basis.shape
    ones = jnp.where(
        lax.broadcasted_iota(jnp.int32, (points, rank), 0) == skel, 1.0, 0.0
    ).astype(BF)
    return jnp.concatenate([basis, ones], axis=1)


def fetch(sources, sems):
    copies = [pltpu.make_async_copy(src, dst, sems.at[j]) for j, (src, dst) in enumerate(sources)]
    for copy in copies:
        copy.start()
    return copies


def pieces_of(ref, count):
    rows = ref.shape[0] // count
    return [ref.at[pl.ds(j * rows, rows)] for j in range(count)]


PIECES = 4


def front_kernel(
    n, order_hbm, skel_hbm, sides_hbm, inverse_hbm, basis_hbm, core_hbm, transfer_hbm, top_hbm, *rest
):
    messages, own_ref = rest[: n - 1], rest[n - 1]
    sides_ref, inverse_ref, gather_ref, pair_ref, top_ref, order_ref = rest[n : n + 6]
    skel_ref, basis_ref, core_ref, transfer_ref, coeffs, sems = rest[n + 6 :]
    me = lax.axis_index("ba")
    points, rank = basis_ref.shape
    rows = points // PIECES
    copies = fetch(
        [(skel_hbm, skel_ref), (basis_hbm, basis_ref), (order_hbm, order_ref)]
        + list(zip(pieces_of(inverse_hbm, PIECES), pieces_of(inverse_ref, PIECES)))
        + [(sides_hbm, sides_ref), (core_hbm, core_ref), (transfer_hbm, transfer_ref), (top_hbm, top_ref)],
        sems,
    )
    share = coeffs.shape[0] // n
    for copy in copies[:3]:
        copy.wait()
    pair_ref[...] = basis_pair(skel_ref[...], basis_ref[...])
    gather_ref[...] = order_columns(order_ref[...], points)
    both = None
    for j in range(PIECES):
        copies[3 + j].wait()
        at = slice(j * rows, (j + 1) * rows)
        part = dot(pair_ref[at, :], inverse_ref[at, :], TN)
        both = part if both is None else both + part
    up = (both[:rank] + both[rank:]).astype(BF)
    up = dot(up, gather_ref[...]).astype(BF)
    for copy in copies[3 + PIECES :]:
        copy.wait()
    coeffs[...] = dot(up, sides_ref[...]).T.astype(BF)
    transfer = transfer_ref[...].astype(BF)

    def block(m):
        return core_ref[:, pl.ds(pl.multiple_of((me ^ m) * rank, rank), rank)]

    for k in range(n):
        out = own_ref if k == 0 else messages[k - 1]
        out[0:share, :] = coeffs[pl.ds(pl.multiple_of((me ^ k) * share, share), share), :]
        out[share : share + rank, :] = transfer
        at = share + rank
        for m in range(n) if k == 0 else [0] + [k ^ m for m in partners(n, k)]:
            out[at : at + rank, :] = block(m)
            at += rank


def applied_kernel(sides_ref, inverse_ref, gather_ref, top_ref, applied_ref, top_out):
    ordered = dot(gather_ref[...], sides_ref[...]).astype(BF)
    applied_ref[...] = dot(inverse_ref[...], ordered).astype(BF)
    top_out[...] = top_ref[...]


def down_kernel(inverse_ref, order_ref, pair_ref, applied_ref, after, applied_out, down_ref):
    del after
    points, rank = down_ref.shape
    placed = order_rows(order_ref[...], points)
    both = dot(inverse_ref[...], pair_ref[...])
    down = (both[:, :rank] + both[:, rank:]).astype(BF)
    applied_out[...] = dot(placed, applied_ref[...]).astype(BF)
    down_ref[...] = dot(placed, down).astype(BF)


def group_kernel(n, rank, after, own_ref, *rest):
    del after
    messages, rest = rest[: n - 1], rest[n - 1 :]
    passed = (len(rest) - 2) // 2
    tops, (level_ref, group_ref), tops_out = rest[:passed], rest[passed : passed + 2], rest[passed + 2 :]
    for top_ref, top_out in zip(tops, tops_out):
        top_out[...] = top_ref[...]
    share = level_ref.shape[0]
    messages = messages[::-1]
    coeffs = [msg[0:share, :] for msg in (own_ref,) + messages]
    transfers = [msg[share : share + rank, :] for msg in (own_ref,) + messages]
    level = [None] * n

    def add(k, term):
        level[k] = term if level[k] is None else level[k] + term

    for k in range(n):
        msg = own_ref if k == 0 else messages[k - 1]
        which = list(range(n)) if k == 0 else [k] + partners(n, k)
        blocks = [msg[share + rank * (j + 1) : share + rank * (j + 2), :] for j in range(len(which))]
        wide = dot(coeffs[k], jnp.concatenate(blocks, axis=1))
        for j, m in enumerate(which):
            add(m, wide[:, j * rank : (j + 1) * rank])
        if len(which) > 1:
            others = jnp.concatenate([coeffs[m] for m in which[1:]], axis=1)
            add(k, dot(others, jnp.concatenate(blocks[1:], axis=1), NT))
    level_ref[...] = jnp.concatenate(level, axis=1)
    rest_of = [(coeffs[k].astype(F32) - level[k]).astype(BF) for k in range(n)]
    total = dot(jnp.concatenate(rest_of, axis=1), jnp.concatenate(transfers, axis=0))
    group_ref[...] = total.astype(BF)


def top_rows_kernel(n, groups, *rest):
    tops, (rows_ref, held) = rest[:n], rest[n:]
    me = lax.axis_index("ba")
    mine = lax.axis_index("aa")
    part = tops[0].shape[0]
    rank = rows_ref.shape[0]
    for k in range(n):
        held[pl.ds(pl.multiple_of((me ^ k) * part, part), part), :] = tops[k][...].astype(F32)
    for m in range(groups):
        rows_ref[:, m * rank : (m + 1) * rank] = held[
            :, pl.ds(pl.multiple_of((mine ^ m) * rank, rank), rank)
        ].astype(BF)


def top_kernel(n, groups, rows_ref, level_ref, *rest):
    messages, pieces, outs = rest[:n], rest[n : n + groups], rest[n + groups :]
    share = level_ref.shape[0]
    rank = rows_ref.shape[0]
    stacked = jnp.concatenate([piece[...] for piece in pieces], axis=1)
    top = dot(stacked, rows_ref[...], NT).astype(BF)
    transfers = jnp.concatenate([msg[share : share + rank, :] for msg in messages], axis=0)
    correction = (level_ref[...] + dot(top, transfers, NT)).astype(BF)
    for k in range(n):
        outs[k][...] = correction[:, k * rank : (k + 1) * rank]


def final_kernel(n, applied_ref, down_ref, *rest):
    pieces, (out_hbm, correction, out_ref, sems) = rest[:n], rest[n:]
    me = lax.axis_index("ba")
    share = pieces[0].shape[0]
    for k in range(n):
        correction[pl.ds(pl.multiple_of((me ^ k) * share, share), share), :] = pieces[k][...]
    rows = out_ref.shape[0] // PIECES
    copies = []
    for j, (src, dst) in enumerate(zip(pieces_of(out_ref, PIECES), pieces_of(out_hbm, PIECES))):
        at = slice(j * rows, (j + 1) * rows)
        out_ref[at, :] = (
            applied_ref[at, :].astype(F32) - dot(down_ref[at, :], correction[...], NT)
        ).astype(BF)
        copies.append(pltpu.make_async_copy(src, dst, sems.at[j]))
        copies[-1].start()
    for copy in copies:
        copy.wait()


def shape(dims, kind=BF):
    return jax.ShapeDtypeStruct(dims, kind)


def call(body, outs, in_specs, out_specs=None, scratch=(), flops=0, moved=0, limit=32):
    return pl.pallas_call(
        body,
        out_shape=outs,
        in_specs=in_specs,
        scratch_shapes=list(scratch),
        compiler_params=pltpu.CompilerParams(vmem_limit_bytes=limit * 1024 * 1024),
        cost_estimate=pl.CostEstimate(flops=flops, bytes_accessed=moved, transcendentals=0),
        **({} if out_specs is None else {"out_specs": out_specs}),
    )


def shards(n, groups, sides, order, skel, inverse, basis, core, transfer, top):
    points, cols = sides.shape
    rank = basis.shape[1]
    share = cols // n
    vmem = pl.BlockSpec(memory_space=pltpu.VMEM)
    hbm = pl.BlockSpec(memory_space=pltpu.HBM)
    unread = pl.BlockSpec(memory_space=pl.ANY)

    def far(*arrays):
        return [pltpu.with_memory_space_constraint(x, pltpu.HBM) for x in arrays]

    def like(array):
        return pltpu.VMEM(array.shape, array.dtype)

    def swap(array, axis, k):
        size = {"aa": groups, "ba": n}[axis]
        return lax.ppermute(array, axis, [(i, i ^ k) for i in range(size)])

    sizes = [share + rank * (2 + len(partners(n, k))) for k in range(1, n)] + [share + rank * (n + 1)]
    *messages, own, sides_held, inverse_held, gather, pair, top_held, order_held = call(
        functools.partial(front_kernel, n),
        [shape((size, rank)) for size in sizes]
        + [shape(sides.shape), shape(inverse.shape)]
        + [shape((points, points)), shape((points, 2 * rank)), shape(top.shape), shape(order.shape, order.dtype)],
        [hbm] * 8,
        scratch=[like(x) for x in (skel, basis, core, transfer)]
        + [pltpu.VMEM((cols, rank), BF), pltpu.SemaphoreType.DMA((7 + PIECES,))],
        flops=2 * rank * points * (3 * points + cols),
        moved=2 * points * (points + cols + rank),
    )(*far(order, skel, sides, inverse, basis, core, transfer, top))
    received = [swap(messages[k - 1], "ba", k) for k in range(1, n)]
    applied, top_held = call(
        applied_kernel,
        [shape((points, cols)), shape(top.shape)],
        [vmem] * 4,
        flops=4 * points * points * cols,
        moved=2 * points * (points + 2 * cols),
    )(sides_held, inverse_held, gather, top_held)
    direct = [1 << j for j in range(n.bit_length() - 1)]
    tops = {k: swap(top_held, "ba", k) for k in direct} | {0: top_held}
    level, group, *passed = call(
        functools.partial(group_kernel, n, rank),
        [shape((share, n * rank), F32), shape((share, rank))] + [shape(top.shape)] * len(direct[:-1]),
        [unread] + [vmem] * (n + len(direct[:-1])),
        flops=2 * share * n * rank * (n + 1) * rank,
        moved=4 * share * n * rank,
    )(applied, own, *received[::-1], *[tops[k] for k in direct[:-1]])
    tops |= dict(zip(direct[:-1], passed))
    for k in range(n):
        if k not in tops:
            high = 1 << (k.bit_length() - 1)
            tops[k] = swap(tops[k ^ high], "ba", high)
    tops = [tops[k] for k in range(n)]
    pieces = {0: group}
    for m in range(2, groups, 2):
        pieces[m] = swap(group, "aa", m)
    for m in range(0, groups, 2):
        pieces[m + 1] = swap(pieces[m], "aa", 1)
    rows = call(
        functools.partial(top_rows_kernel, n, groups),
        shape((rank, groups * rank)),
        [vmem] * n,
        scratch=[pltpu.VMEM((rank, groups * rank), F32)],
        moved=rank,
    )(*tops)
    corrections = call(
        functools.partial(top_kernel, n, groups),
        [shape((share, rank))] * n,
        [vmem] * (2 + n + groups),
        flops=2 * share * rank * (groups + n) * rank,
        moved=4 * share * n * rank,
    )(rows, level, own, *received, *[pieces[m] for m in range(groups)])
    back = [corrections[0]] + [swap(corrections[k], "ba", k) for k in range(1, n)]
    applied, down = call(
        down_kernel,
        [shape((points, cols)), shape((points, rank))],
        [vmem] * 4 + [unread],
        flops=2 * points * points * (3 * rank + cols),
        moved=2 * points * (points + 2 * cols),
    )(inverse_held, order_held, pair, applied, corrections[0])
    return call(
        functools.partial(final_kernel, n),
        shape((points, cols)),
        [vmem] * (2 + n),
        out_specs=hbm,
        scratch=[pltpu.VMEM((cols, rank), BF), pltpu.VMEM((points, cols), BF), pltpu.SemaphoreType.DMA((PIECES,))],
        flops=2 * points * cols * rank,
        moved=4 * points * cols,
    )(applied, down, *back)


def solution(mesh):
    spec = P(("aa", "ba"), None)
    return jax.shard_map(
        functools.partial(shards, mesh.shape["ba"], mesh.shape["aa"]),
        mesh=mesh,
        in_specs=(spec,) * 8,
        out_specs=spec,
        check_vma=False,
    )
```

```python
import functools

import jax
import jax.numpy as jnp
from jax import lax
from jax.experimental import pallas as pl
from jax.experimental.pallas import tpu as pltpu
from jax.sharding import PartitionSpec as P

BF = jnp.bfloat16
F32 = jnp.float32
NN = (((1,), (0,)), ((), ()))
NT = (((1,), (1,)), ((), ()))
TN = (((0,), (0,)), ((), ()))


def dot(a, b, dims=NN):
    return lax.dot_general(a, b, dims, preferred_element_type=F32)


def partners(n, k):
    half = (n - 2) // 2
    return [(k - 1 + j) % (n - 1) + 1 for j in range(1, half + 1)]


def column_of(row, count):
    wide = jnp.broadcast_to(row.astype(F32), (count, row.shape[1]))
    return wide.T.astype(jnp.int32)


def order_rows(order, size):
    return jnp.where(
        lax.broadcasted_iota(jnp.int32, (size, size), 0) == order, 1.0, 0.0
    ).astype(BF)


def order_columns(order, size):
    column = column_of(order, 128)
    lanes = lax.broadcasted_iota(jnp.int32, (size, 128), 1)
    return jnp.concatenate(
        [jnp.where(column == lanes + j * 128, 1.0, 0.0).astype(BF) for j in range(size // 128)], axis=1
    )


def basis_pair(skel, basis):
    points, rank = basis.shape
    ones = jnp.where(
        lax.broadcasted_iota(jnp.int32, (points, rank), 0) == skel, 1.0, 0.0
    ).astype(BF)
    return jnp.concatenate([basis, ones], axis=1)


def fetch(sources, sems):
    copies = [pltpu.make_async_copy(src, dst, sems.at[j]) for j, (src, dst) in enumerate(sources)]
    for copy in copies:
        copy.start()
    return copies


def pieces_of(ref, count):
    rows = ref.shape[0] // count
    return [ref.at[pl.ds(j * rows, rows)] for j in range(count)]


PIECES = 4


def pack_kernel(n, core_hbm, transfer_hbm, top_hbm, *rest):
    messages, own_ref = rest[: n - 1], rest[n - 1]
    core_ref, transfer_ref, top_ref, sems = rest[n:]
    me = lax.axis_index("ba")
    rank = transfer_ref.shape[0]
    for copy in fetch([(core_hbm, core_ref), (transfer_hbm, transfer_ref), (top_hbm, top_ref)], sems):
        copy.wait()
    transfer = transfer_ref[...].astype(BF)
    groups = top_ref.shape[1] // rank
    top = top_ref[...].astype(F32)
    top = jnp.concatenate([top[:, g * rank : (g + 1) * rank] for g in range(groups)], axis=0).astype(BF)
    for k in range(n):
        out = own_ref if k == 0 else messages[k - 1]
        out[0:rank, :] = transfer
        at = rank
        for m in range(n) if k == 0 else [0] + [k ^ m for m in partners(n, k)]:
            out[at : at + rank, :] = core_ref[:, pl.ds(pl.multiple_of((me ^ m) * rank, rank), rank)]
            at += rank
        out[at:, :] = top


def front_kernel(n, order_ref, skel_ref, sides_ref, inverse_ref, basis_ref, after, *rest):
    del after
    outs, (gather_ref, pair_ref, coeffs) = rest[:n], rest[n:]
    me = lax.axis_index("ba")
    points, rank = basis_ref.shape
    share = outs[0].shape[0]
    pair = basis_pair(skel_ref[...], basis_ref[...])
    both = dot(pair, inverse_ref[...], TN)
    gather = order_columns(order_ref[...], points)
    up = (both[:rank] + both[rank:]).astype(BF)
    up = dot(up, gather).astype(BF)
    coeffs[...] = dot(up, sides_ref[...]).T.astype(BF)
    for k in range(n):
        outs[k][...] = coeffs[pl.ds(pl.multiple_of((me ^ k) * share, share), share), :]
    gather_ref[...] = gather
    pair_ref[...] = pair


def ordered_kernel(sides_ref, gather_ref, ordered_ref):
    ordered_ref[...] = dot(gather_ref[...], sides_ref[...]).astype(BF)


def applied_kernel(inverse_ref, ordered_ref, group_ref, applied_ref, group_out):
    applied_ref[...] = dot(inverse_ref[...], ordered_ref[...]).astype(BF)
    group_out[...] = group_ref[...]


def down_kernel(inverse_ref, order_ref, pair_ref, applied_ref, after, applied_out, down_ref):
    del after
    points, rank = down_ref.shape
    placed = order_rows(order_ref[...], points)
    both = dot(inverse_ref[...], pair_ref[...])
    down = (both[:, :rank] + both[:, rank:]).astype(BF)
    applied_out[...] = dot(placed, applied_ref[...]).astype(BF)
    down_ref[...] = dot(placed, down).astype(BF)


def group_kernel(n, rank, after, *rest):
    del after
    pieces, messages, (level_ref, group_ref) = rest[:n][::-1], rest[n : 2 * n][::-1], rest[2 * n :]
    coeffs = [piece[...] for piece in pieces]
    transfers = [msg[0:rank, :] for msg in messages]
    level = [None] * n

    def add(k, term):
        level[k] = term if level[k] is None else level[k] + term

    for k in range(n):
        which = list(range(n)) if k == 0 else [k] + partners(n, k)
        blocks = [messages[k][rank * (j + 1) : rank * (j + 2), :] for j in range(len(which))]
        wide = dot(coeffs[k], jnp.concatenate(blocks, axis=1))
        for j, m in enumerate(which):
            add(m, wide[:, j * rank : (j + 1) * rank])
        if len(which) > 1:
            others = jnp.concatenate([coeffs[m] for m in which[1:]], axis=1)
            add(k, dot(others, jnp.concatenate(blocks[1:], axis=1), NT))
    level_ref[...] = jnp.concatenate(level, axis=1)
    rest_of = [(coeffs[k].astype(F32) - level[k]).astype(BF) for k in range(n)]
    total = dot(jnp.concatenate(rest_of, axis=1), jnp.concatenate(transfers, axis=0))
    group_ref[...] = total.astype(BF)


def top_rows_kernel(n, groups, *rest):
    messages, (coeffs_ref, coeffs_out, rows_ref, held) = rest[:n], rest[n:]
    coeffs_out[...] = coeffs_ref[...]
    me = lax.axis_index("ba")
    mine = lax.axis_index("aa")
    rank = rows_ref.shape[0]
    part = rank // n
    for k in range(n):
        tail = messages[k][messages[k].shape[0] - groups * part :, :].astype(F32)
        for g in range(groups):
            held[pl.ds(pl.multiple_of((me ^ k) * part, part), part), g * rank : (g + 1) * rank] = tail[
                g * part : (g + 1) * part
            ]
    for m in range(groups):
        rows_ref[:, m * rank : (m + 1) * rank] = held[
            :, pl.ds(pl.multiple_of((mine ^ m) * rank, rank), rank)
        ].astype(BF)


def top_kernel(n, groups, rows_ref, level_ref, *rest):
    messages, pieces, outs = rest[:n], rest[n : n + groups], rest[n + groups :]
    rank = rows_ref.shape[0]
    stacked = jnp.concatenate([piece[...] for piece in pieces], axis=1)
    top = dot(stacked, rows_ref[...], NT).astype(BF)
    transfers = jnp.concatenate([msg[0:rank, :] for msg in messages], axis=0)
    correction = (level_ref[...] + dot(top, transfers, NT)).astype(BF)
    for k in range(n):
        outs[k][...] = correction[:, k * rank : (k + 1) * rank]


def final_kernel(n, applied_ref, down_ref, *rest):
    pieces, (out_hbm, correction, out_ref, sems) = rest[:n], rest[n:]
    me = lax.axis_index("ba")
    share = pieces[0].shape[0]
    for k in range(n):
        correction[pl.ds(pl.multiple_of((me ^ k) * share, share), share), :] = pieces[k][...]
    rows = out_ref.shape[0] // PIECES
    copies = []
    for j, (src, dst) in enumerate(zip(pieces_of(out_ref, PIECES), pieces_of(out_hbm, PIECES))):
        at = slice(j * rows, (j + 1) * rows)
        out_ref[at, :] = (
            applied_ref[at, :].astype(F32) - dot(down_ref[at, :], correction[...], NT)
        ).astype(BF)
        copies.append(pltpu.make_async_copy(src, dst, sems.at[j]))
        copies[-1].start()
    for copy in copies:
        copy.wait()


def shape(dims, kind=BF):
    return jax.ShapeDtypeStruct(dims, kind)


def call(body, outs, in_specs, out_specs=None, scratch=(), flops=0, moved=0, limit=32):
    return pl.pallas_call(
        body,
        out_shape=outs,
        in_specs=in_specs,
        scratch_shapes=list(scratch),
        compiler_params=pltpu.CompilerParams(vmem_limit_bytes=limit * 1024 * 1024),
        cost_estimate=pl.CostEstimate(flops=flops, bytes_accessed=moved, transcendentals=0),
        **({} if out_specs is None else {"out_specs": out_specs}),
    )


def shards(n, groups, sides, order, skel, inverse, basis, core, transfer, top):
    points, cols = sides.shape
    rank = basis.shape[1]
    share = cols // n
    vmem = pl.BlockSpec(memory_space=pltpu.VMEM)
    hbm = pl.BlockSpec(memory_space=pltpu.HBM)
    unread = pl.BlockSpec(memory_space=pl.ANY)

    def far(*arrays):
        return [pltpu.with_memory_space_constraint(x, pltpu.HBM) for x in arrays]

    def like(array):
        return pltpu.VMEM(array.shape, array.dtype)

    def swap(array, axis, k):
        size = {"aa": groups, "ba": n}[axis]
        return lax.ppermute(array, axis, [(i, i ^ k) for i in range(size)])

    tail = groups * top.shape[0]
    sizes = [rank * (2 + len(partners(n, k))) + tail for k in range(1, n)] + [rank * (n + 1) + tail]
    *messages, own = call(
        functools.partial(pack_kernel, n),
        [shape((size, rank)) for size in sizes],
        [hbm] * 3,
        scratch=[like(x) for x in (core, transfer, top)] + [pltpu.SemaphoreType.DMA((3,))],
        flops=16 * points * points * points,
        moved=16 * points * (points + cols + rank),
    )(*far(core, transfer, top))
    received = [own] + [swap(messages[k - 1], "ba", k) for k in range(1, n)]
    *coeffs, gather, pair = call(
        functools.partial(front_kernel, n),
        [shape((share, rank))] * n + [shape((points, points)), shape((points, 2 * rank))],
        [vmem] * 5 + [unread],
        scratch=[pltpu.VMEM((cols, rank), BF)],
        flops=2 * rank * points * (3 * points + cols),
        moved=2 * points * (points + cols + rank),
    )(order, skel, sides, inverse, basis, own)
    coeffs[1], rows = call(
        functools.partial(top_rows_kernel, n, groups),
        [shape((share, rank)), shape((rank, groups * rank))],
        [vmem] * (n + 1),
        scratch=[pltpu.VMEM((rank, groups * rank), F32)],
        moved=4 * rank * groups * rank,
    )(*received, coeffs[1])
    coeffs = [coeffs[0]] + [swap(coeffs[k], "ba", k) for k in range(1, n)]
    ordered = call(
        ordered_kernel,
        shape((points, cols)),
        [vmem] * 2,
        flops=2 * points * points * cols,
        moved=2 * points * (points + 2 * cols),
    )(sides, gather)
    level, group = call(
        functools.partial(group_kernel, n, rank),
        [shape((share, n * rank), F32), shape((share, rank))],
        [unread] + [vmem] * (2 * n),
        flops=2 * share * n * rank * (n + 1) * rank,
        moved=4 * share * n * rank,
    )(ordered, *coeffs[::-1], *received[::-1])
    applied, group_held = call(
        applied_kernel,
        [shape((points, cols)), shape((share, rank))],
        [vmem] * 3,
        flops=2 * points * points * cols,
        moved=2 * points * (points + 2 * cols),
    )(inverse, ordered, group)
    pieces = {0: group}
    for m in range(2, groups, 2):
        pieces[m] = swap(group, "aa", m)
    for m in range(0, groups, 2):
        pieces[m + 1] = swap(pieces[m] if m else group_held, "aa", 1)
    corrections = call(
        functools.partial(top_kernel, n, groups),
        [shape((share, rank))] * n,
        [vmem] * (2 + n + groups),
        flops=2 * share * rank * (groups + n) * rank,
        moved=4 * share * n * rank,
    )(rows, level, *received, *[pieces[m] for m in range(groups)])
    back = [corrections[0]] + [swap(corrections[k], "ba", k) for k in range(1, n)]
    applied, down = call(
        down_kernel,
        [shape((points, cols)), shape((points, rank))],
        [vmem] * 4 + [unread],
        flops=2 * points * points * (3 * rank + cols),
        moved=2 * points * (points + 2 * cols),
    )(inverse, order, pair, applied, corrections[0])
    return call(
        functools.partial(final_kernel, n),
        shape((points, cols)),
        [vmem] * (2 + n),
        out_specs=hbm,
        scratch=[pltpu.VMEM((cols, rank), BF), pltpu.VMEM((points, cols), BF), pltpu.SemaphoreType.DMA((PIECES,))],
        flops=2 * points * cols * rank,
        moved=4 * points * cols,
    )(applied, down, *back)


def solution(mesh):
    spec = P(("aa", "ba"), None)
    return jax.shard_map(
        functools.partial(shards, mesh.shape["ba"], mesh.shape["aa"]),
        mesh=mesh,
        in_specs=(spec,) * 8,
        out_specs=spec,
        check_vma=False,
    )
```

```python
import functools

import jax
import jax.numpy as jnp
from jax import lax
from jax.experimental import pallas as pl
from jax.experimental.pallas import tpu as pltpu
from jax.sharding import PartitionSpec as P

BF = jnp.bfloat16
F32 = jnp.float32
NN = (((1,), (0,)), ((), ()))
NT = (((1,), (1,)), ((), ()))
TN = (((0,), (0,)), ((), ()))


def dot(a, b, dims=NN):
    return lax.dot_general(a, b, dims, preferred_element_type=F32)


def partners(n, k):
    half = (n - 2) // 2
    return [(k - 1 + j) % (n - 1) + 1 for j in range(1, half + 1)]


def column_of(row, count):
    wide = jnp.broadcast_to(row.astype(F32), (count, row.shape[1]))
    return wide.T.astype(jnp.int32)


def order_rows(order, size):
    return jnp.where(
        lax.broadcasted_iota(jnp.int32, (size, size), 0) == order, 1.0, 0.0
    ).astype(BF)


def order_columns(order, size):
    column = column_of(order, 128)
    lanes = lax.broadcasted_iota(jnp.int32, (size, 128), 1)
    return jnp.concatenate(
        [jnp.where(column == lanes + j * 128, 1.0, 0.0).astype(BF) for j in range(size // 128)], axis=1
    )


def basis_pair(skel, basis):
    points, rank = basis.shape
    ones = jnp.where(
        lax.broadcasted_iota(jnp.int32, (points, rank), 0) == skel, 1.0, 0.0
    ).astype(BF)
    return jnp.concatenate([basis, ones], axis=1)


def fetch(sources, sems):
    copies = [pltpu.make_async_copy(src, dst, sems.at[j]) for j, (src, dst) in enumerate(sources)]
    for copy in copies:
        copy.start()
    return copies


def pieces_of(ref, count):
    rows = ref.shape[0] // count
    return [ref.at[pl.ds(j * rows, rows)] for j in range(count)]


PIECES = 4


def front_kernel(
    n, order_hbm, skel_hbm, sides_hbm, inverse_hbm, basis_hbm, core_hbm, transfer_hbm, top_hbm, *rest
):
    messages, own_ref = rest[: n - 1], rest[n - 1]
    sides_ref, inverse_ref, gather_ref, pair_ref, top_ref, order_ref = rest[n : n + 6]
    skel_ref, basis_ref, core_ref, transfer_ref, coeffs, sems = rest[n + 6 :]
    me = lax.axis_index("ba")
    points, rank = basis_ref.shape
    rows = points // PIECES
    copies = fetch(
        [(skel_hbm, skel_ref), (basis_hbm, basis_ref), (order_hbm, order_ref)]
        + list(zip(pieces_of(inverse_hbm, PIECES), pieces_of(inverse_ref, PIECES)))
        + [(sides_hbm, sides_ref), (core_hbm, core_ref), (transfer_hbm, transfer_ref), (top_hbm, top_ref)],
        sems,
    )
    share = coeffs.shape[0] // n
    for copy in copies[:3]:
        copy.wait()
    pair_ref[...] = basis_pair(skel_ref[...], basis_ref[...])
    gather_ref[...] = order_columns(order_ref[...], points)
    both = None
    for j in range(PIECES):
        copies[3 + j].wait()
        at = slice(j * rows, (j + 1) * rows)
        part = dot(pair_ref[at, :], inverse_ref[at, :], TN)
        both = part if both is None else both + part
    up = (both[:rank] + both[rank:]).astype(BF)
    up = dot(up, gather_ref[...]).astype(BF)
    for copy in copies[3 + PIECES :]:
        copy.wait()
    coeffs[...] = dot(up, sides_ref[...]).T.astype(BF)
    transfer = transfer_ref[...].astype(BF)

    def block(m):
        return core_ref[:, pl.ds(pl.multiple_of((me ^ m) * rank, rank), rank)]

    for k in range(n):
        out = own_ref if k == 0 else messages[k - 1]
        out[0:share, :] = coeffs[pl.ds(pl.multiple_of((me ^ k) * share, share), share), :]
        out[share : share + rank, :] = transfer
        at = share + rank
        for m in range(n) if k == 0 else [0] + [k ^ m for m in partners(n, k)]:
            out[at : at + rank, :] = block(m)
            at += rank


def applied_kernel(sides_ref, inverse_ref, gather_ref, top_ref, applied_ref, top_out):
    ordered = dot(gather_ref[...], sides_ref[...]).astype(BF)
    applied_ref[...] = dot(inverse_ref[...], ordered).astype(BF)
    top_out[...] = top_ref[...]


def down_kernel(inverse_ref, order_ref, pair_ref, applied_ref, after, applied_out, down_ref):
    del after
    points, rank = down_ref.shape
    placed = order_rows(order_ref[...], points)
    both = dot(inverse_ref[...], pair_ref[...])
    down = (both[:, :rank] + both[:, rank:]).astype(BF)
    applied_out[...] = dot(placed, applied_ref[...]).astype(BF)
    down_ref[...] = dot(placed, down).astype(BF)


def group_kernel(n, rank, after, own_ref, *rest):
    del after
    messages, (level_ref, group_ref) = rest[: n - 1], rest[n - 1 :]
    share = level_ref.shape[0]
    messages = messages[::-1]
    coeffs = [msg[0:share, :] for msg in (own_ref,) + messages]
    transfers = [msg[share : share + rank, :] for msg in (own_ref,) + messages]
    level = [None] * n

    def add(k, term):
        level[k] = term if level[k] is None else level[k] + term

    for k in range(n):
        msg = own_ref if k == 0 else messages[k - 1]
        which = list(range(n)) if k == 0 else [k] + partners(n, k)
        blocks = [msg[share + rank * (j + 1) : share + rank * (j + 2), :] for j in range(len(which))]
        wide = dot(coeffs[k], jnp.concatenate(blocks, axis=1))
        for j, m in enumerate(which):
            add(m, wide[:, j * rank : (j + 1) * rank])
        if len(which) > 1:
            others = jnp.concatenate([coeffs[m] for m in which[1:]], axis=1)
            add(k, dot(others, jnp.concatenate(blocks[1:], axis=1), NT))
    level_ref[...] = jnp.concatenate(level, axis=1)
    rest_of = [(coeffs[k].astype(F32) - level[k]).astype(BF) for k in range(n)]
    total = dot(jnp.concatenate(rest_of, axis=1), jnp.concatenate(transfers, axis=0))
    group_ref[...] = total.astype(BF)


def top_rows_kernel(n, groups, *rest):
    tops, (rows_ref, held) = rest[:n], rest[n:]
    me = lax.axis_index("ba")
    mine = lax.axis_index("aa")
    part = tops[0].shape[0]
    rank = rows_ref.shape[0]
    for k in range(n):
        held[pl.ds(pl.multiple_of((me ^ k) * part, part), part), :] = tops[k][...].astype(F32)
    for m in range(groups):
        rows_ref[:, m * rank : (m + 1) * rank] = held[
            :, pl.ds(pl.multiple_of((mine ^ m) * rank, rank), rank)
        ].astype(BF)


def top_kernel(n, groups, rows_ref, level_ref, *rest):
    messages, pieces, outs = rest[:n], rest[n : n + groups], rest[n + groups :]
    share = level_ref.shape[0]
    rank = rows_ref.shape[0]
    stacked = jnp.concatenate([piece[...] for piece in pieces], axis=1)
    top = dot(stacked, rows_ref[...], NT).astype(BF)
    transfers = jnp.concatenate([msg[share : share + rank, :] for msg in messages], axis=0)
    correction = (level_ref[...] + dot(top, transfers, NT)).astype(BF)
    for k in range(n):
        outs[k][...] = correction[:, k * rank : (k + 1) * rank]


def final_kernel(n, applied_ref, down_ref, *rest):
    pieces, (out_hbm, correction, out_ref, sems) = rest[:n][::-1], rest[n:]
    me = lax.axis_index("ba")
    share = pieces[0].shape[0]
    for k in range(n):
        correction[pl.ds(pl.multiple_of((me ^ k) * share, share), share), :] = pieces[k][...]
    rows = out_ref.shape[0] // PIECES
    copies = []
    for j, (src, dst) in enumerate(zip(pieces_of(out_ref, PIECES), pieces_of(out_hbm, PIECES))):
        at = slice(j * rows, (j + 1) * rows)
        out_ref[at, :] = (
            applied_ref[at, :].astype(F32) - dot(down_ref[at, :], correction[...], NT)
        ).astype(BF)
        copies.append(pltpu.make_async_copy(src, dst, sems.at[j]))
        copies[-1].start()
    for copy in copies:
        copy.wait()


def shape(dims, kind=BF):
    return jax.ShapeDtypeStruct(dims, kind)


def call(body, outs, in_specs, out_specs=None, scratch=(), flops=0, moved=0, limit=32):
    return pl.pallas_call(
        body,
        out_shape=outs,
        in_specs=in_specs,
        scratch_shapes=list(scratch),
        compiler_params=pltpu.CompilerParams(vmem_limit_bytes=limit * 1024 * 1024),
        cost_estimate=pl.CostEstimate(flops=flops, bytes_accessed=moved, transcendentals=0),
        **({} if out_specs is None else {"out_specs": out_specs}),
    )


def shards(n, groups, sides, order, skel, inverse, basis, core, transfer, top):
    points, cols = sides.shape
    rank = basis.shape[1]
    share = cols // n
    vmem = pl.BlockSpec(memory_space=pltpu.VMEM)
    hbm = pl.BlockSpec(memory_space=pltpu.HBM)
    unread = pl.BlockSpec(memory_space=pl.ANY)

    def far(*arrays):
        return [pltpu.with_memory_space_constraint(x, pltpu.HBM) for x in arrays]

    def like(array):
        return pltpu.VMEM(array.shape, array.dtype)

    def swap(array, axis, k):
        size = {"aa": groups, "ba": n}[axis]
        return lax.ppermute(array, axis, [(i, i ^ k) for i in range(size)])

    sizes = [share + rank * (2 + len(partners(n, k))) for k in range(1, n)] + [share + rank * (n + 1)]
    *messages, own, sides_held, inverse_held, gather, pair, top_held, order_held = call(
        functools.partial(front_kernel, n),
        [shape((size, rank)) for size in sizes]
        + [shape(sides.shape), shape(inverse.shape)]
        + [shape((points, points)), shape((points, 2 * rank)), shape(top.shape), shape(order.shape, order.dtype)],
        [hbm] * 8,
        scratch=[like(x) for x in (skel, basis, core, transfer)]
        + [pltpu.VMEM((cols, rank), BF), pltpu.SemaphoreType.DMA((7 + PIECES,))],
        flops=2 * rank * points * (3 * points + cols),
        moved=2 * points * (points + cols + rank),
    )(*far(order, skel, sides, inverse, basis, core, transfer, top))
    received = [swap(messages[k - 1], "ba", k) for k in range(1, n)]
    applied, top_held = call(
        applied_kernel,
        [shape((points, cols)), shape(top.shape)],
        [vmem] * 4,
        flops=4 * points * points * cols,
        moved=2 * points * (points + 2 * cols),
    )(sides_held, inverse_held, gather, top_held)
    tops = [top_held] + [swap(top_held, "ba", k) for k in range(1, n)]
    level, group = call(
        functools.partial(group_kernel, n, rank),
        [shape((share, n * rank), F32), shape((share, rank))],
        [unread] + [vmem] * n,
        flops=2 * share * n * rank * (n + 1) * rank,
        moved=4 * share * n * rank,
    )(applied, own, *received[::-1])
    pieces = {0: group}
    for m in range(2, groups, 2):
        pieces[m] = swap(group, "aa", m)
    for m in range(0, groups, 2):
        pieces[m + 1] = swap(pieces[m], "aa", 1)
    rows = call(
        functools.partial(top_rows_kernel, n, groups),
        shape((rank, groups * rank)),
        [vmem] * n,
        scratch=[pltpu.VMEM((rank, groups * rank), F32)],
        moved=4 * rank * groups * rank,
    )(*tops)
    corrections = call(
        functools.partial(top_kernel, n, groups),
        [shape((share, rank))] * n,
        [vmem] * (2 + n + groups),
        flops=2 * share * rank * (groups + n) * rank,
        moved=4 * share * n * rank,
    )(rows, level, own, *received, *[pieces[m] for m in range(groups)])
    back = [corrections[0]] + [swap(corrections[k], "ba", k) for k in range(1, n)]
    applied, down = call(
        down_kernel,
        [shape((points, cols)), shape((points, rank))],
        [vmem] * 4 + [unread],
        flops=2 * points * points * (3 * rank + cols),
        moved=2 * points * (points + 2 * cols),
    )(inverse_held, order_held, pair, applied, corrections[0])
    return call(
        functools.partial(final_kernel, n),
        shape((points, cols)),
        [vmem] * (2 + n),
        out_specs=hbm,
        scratch=[pltpu.VMEM((cols, rank), BF), pltpu.VMEM((points, cols), BF), pltpu.SemaphoreType.DMA((PIECES,))],
        flops=2 * points * cols * rank,
        moved=4 * points * cols,
    )(applied, down, *back[::-1])


def solution(mesh):
    spec = P(("aa", "ba"), None)
    return jax.shard_map(
        functools.partial(shards, mesh.shape["ba"], mesh.shape["aa"]),
        mesh=mesh,
        in_specs=(spec,) * 8,
        out_specs=spec,
        check_vma=False,
    )
```

```python
import functools

import jax
import jax.numpy as jnp
from jax import lax
from jax.experimental import pallas as pl
from jax.experimental.pallas import tpu as pltpu
from jax.sharding import PartitionSpec as P

BF = jnp.bfloat16
F32 = jnp.float32
NN = (((1,), (0,)), ((), ()))
NT = (((1,), (1,)), ((), ()))
TN = (((0,), (0,)), ((), ()))


def dot(a, b, dims=NN):
    return lax.dot_general(a, b, dims, preferred_element_type=F32)


def partners(n, k):
    half = (n - 2) // 2
    return [(k - 1 + j) % (n - 1) + 1 for j in range(1, half + 1)]


def column_of(row, count):
    wide = jnp.broadcast_to(row.astype(F32), (count, row.shape[1]))
    return wide.T.astype(jnp.int32)


def order_rows(order, size):
    return jnp.where(
        lax.broadcasted_iota(jnp.int32, (size, size), 0) == order, 1.0, 0.0
    ).astype(BF)


def order_columns(order, size):
    column = column_of(order, 128)
    lanes = lax.broadcasted_iota(jnp.int32, (size, 128), 1)
    return jnp.concatenate(
        [jnp.where(column == lanes + j * 128, 1.0, 0.0).astype(BF) for j in range(size // 128)], axis=1
    )


def basis_pair(skel, basis):
    points, rank = basis.shape
    ones = jnp.where(
        lax.broadcasted_iota(jnp.int32, (points, rank), 0) == skel, 1.0, 0.0
    ).astype(BF)
    return jnp.concatenate([basis, ones], axis=1)


def fetch(sources, sems):
    copies = [pltpu.make_async_copy(src, dst, sems.at[j]) for j, (src, dst) in enumerate(sources)]
    for copy in copies:
        copy.start()
    return copies


def pieces_of(ref, count):
    rows = ref.shape[0] // count
    return [ref.at[pl.ds(j * rows, rows)] for j in range(count)]


PIECES = 4


def front_kernel(
    n, order_hbm, skel_hbm, sides_hbm, inverse_hbm, basis_hbm, core_hbm, transfer_hbm, top_hbm, *rest
):
    messages, own_ref = rest[: n - 1], rest[n - 1]
    sides_ref, inverse_ref, gather_ref, pair_ref, top_ref, order_ref = rest[n : n + 6]
    skel_ref, basis_ref, core_ref, transfer_ref, coeffs, sems = rest[n + 6 :]
    me = lax.axis_index("ba")
    points, rank = basis_ref.shape
    rows = points // PIECES
    copies = fetch(
        [(skel_hbm, skel_ref), (basis_hbm, basis_ref), (order_hbm, order_ref)]
        + list(zip(pieces_of(inverse_hbm, PIECES), pieces_of(inverse_ref, PIECES)))
        + [(sides_hbm, sides_ref), (core_hbm, core_ref), (transfer_hbm, transfer_ref), (top_hbm, top_ref)],
        sems,
    )
    share = coeffs.shape[0] // n
    for copy in copies[:3]:
        copy.wait()
    pair_ref[...] = basis_pair(skel_ref[...], basis_ref[...])
    gather_ref[...] = order_columns(order_ref[...], points)
    both = None
    for j in range(PIECES):
        copies[3 + j].wait()
        at = slice(j * rows, (j + 1) * rows)
        part = dot(pair_ref[at, :], inverse_ref[at, :], TN)
        both = part if both is None else both + part
    up = (both[:rank] + both[rank:]).astype(BF)
    up = dot(up, gather_ref[...]).astype(BF)
    for copy in copies[3 + PIECES :]:
        copy.wait()
    coeffs[...] = dot(up, sides_ref[...]).T.astype(BF)
    transfer = transfer_ref[...].astype(BF)

    def block(m):
        return core_ref[:, pl.ds(pl.multiple_of((me ^ m) * rank, rank), rank)]

    for k in range(n):
        out = own_ref if k == 0 else messages[k - 1]
        out[0:share, :] = coeffs[pl.ds(pl.multiple_of((me ^ k) * share, share), share), :]
        out[share : share + rank, :] = transfer
        at = share + rank
        for m in range(n) if k == 0 else [0] + [k ^ m for m in partners(n, k)]:
            out[at : at + rank, :] = block(m)
            at += rank


def ordered_kernel(sides_ref, gather_ref, top_ref, ordered_ref, top_out):
    ordered_ref[...] = dot(gather_ref[...], sides_ref[...]).astype(BF)
    top_out[...] = top_ref[...]


def applied_kernel(inverse_ref, ordered_ref, group_ref, applied_ref, group_out):
    applied_ref[...] = dot(inverse_ref[...], ordered_ref[...]).astype(BF)
    group_out[...] = group_ref[...]


def down_kernel(inverse_ref, order_ref, pair_ref, applied_ref, after, applied_out, down_ref):
    del after
    points, rank = down_ref.shape
    placed = order_rows(order_ref[...], points)
    both = dot(inverse_ref[...], pair_ref[...])
    down = (both[:, :rank] + both[:, rank:]).astype(BF)
    applied_out[...] = dot(placed, applied_ref[...]).astype(BF)
    down_ref[...] = dot(placed, down).astype(BF)


def group_kernel(n, rank, after, own_ref, *rest):
    del after
    messages, (level_ref, group_ref) = rest[: n - 1], rest[n - 1 :]
    share = level_ref.shape[0]
    messages = messages[::-1]
    coeffs = [msg[0:share, :] for msg in (own_ref,) + messages]
    transfers = [msg[share : share + rank, :] for msg in (own_ref,) + messages]
    level = [None] * n

    def add(k, term):
        level[k] = term if level[k] is None else level[k] + term

    for k in range(n):
        msg = own_ref if k == 0 else messages[k - 1]
        which = list(range(n)) if k == 0 else [k] + partners(n, k)
        blocks = [msg[share + rank * (j + 1) : share + rank * (j + 2), :] for j in range(len(which))]
        wide = dot(coeffs[k], jnp.concatenate(blocks, axis=1))
        for j, m in enumerate(which):
            add(m, wide[:, j * rank : (j + 1) * rank])
        if len(which) > 1:
            others = jnp.concatenate([coeffs[m] for m in which[1:]], axis=1)
            add(k, dot(others, jnp.concatenate(blocks[1:], axis=1), NT))
    level_ref[...] = jnp.concatenate(level, axis=1)
    rest_of = [(coeffs[k].astype(F32) - level[k]).astype(BF) for k in range(n)]
    total = dot(jnp.concatenate(rest_of, axis=1), jnp.concatenate(transfers, axis=0))
    group_ref[...] = total.astype(BF)


def top_rows_kernel(n, groups, *rest):
    tops, (rows_ref, held) = rest[:n][::-1], rest[n:]
    me = lax.axis_index("ba")
    mine = lax.axis_index("aa")
    part = tops[0].shape[0]
    rank = rows_ref.shape[0]
    for k in range(n):
        held[pl.ds(pl.multiple_of((me ^ k) * part, part), part), :] = tops[k][...].astype(F32)
    for m in range(groups):
        rows_ref[:, m * rank : (m + 1) * rank] = held[
            :, pl.ds(pl.multiple_of((mine ^ m) * rank, rank), rank)
        ].astype(BF)


def top_kernel(n, groups, rows_ref, level_ref, *rest):
    messages, pieces, outs = rest[:n], rest[n : n + groups], rest[n + groups :]
    share = level_ref.shape[0]
    rank = rows_ref.shape[0]
    stacked = jnp.concatenate([piece[...] for piece in pieces], axis=1)
    top = dot(stacked, rows_ref[...], NT).astype(BF)
    transfers = jnp.concatenate([msg[share : share + rank, :] for msg in messages], axis=0)
    correction = (level_ref[...] + dot(top, transfers, NT)).astype(BF)
    for k in range(n):
        outs[k][...] = correction[:, k * rank : (k + 1) * rank]


def final_kernel(n, applied_ref, down_ref, *rest):
    pieces, (out_hbm, correction, out_ref, sems) = rest[:n][::-1], rest[n:]
    me = lax.axis_index("ba")
    share = pieces[0].shape[0]
    for k in range(n):
        correction[pl.ds(pl.multiple_of((me ^ k) * share, share), share), :] = pieces[k][...]
    rows = out_ref.shape[0] // PIECES
    copies = []
    for j, (src, dst) in enumerate(zip(pieces_of(out_ref, PIECES), pieces_of(out_hbm, PIECES))):
        at = slice(j * rows, (j + 1) * rows)
        out_ref[at, :] = (
            applied_ref[at, :].astype(F32) - dot(down_ref[at, :], correction[...], NT)
        ).astype(BF)
        copies.append(pltpu.make_async_copy(src, dst, sems.at[j]))
        copies[-1].start()
    for copy in copies:
        copy.wait()


def shape(dims, kind=BF):
    return jax.ShapeDtypeStruct(dims, kind)


def call(body, outs, in_specs, out_specs=None, scratch=(), flops=0, moved=0, limit=32):
    return pl.pallas_call(
        body,
        out_shape=outs,
        in_specs=in_specs,
        scratch_shapes=list(scratch),
        compiler_params=pltpu.CompilerParams(vmem_limit_bytes=limit * 1024 * 1024),
        cost_estimate=pl.CostEstimate(flops=flops, bytes_accessed=moved, transcendentals=0),
        **({} if out_specs is None else {"out_specs": out_specs}),
    )


def shards(n, groups, sides, order, skel, inverse, basis, core, transfer, top):
    points, cols = sides.shape
    rank = basis.shape[1]
    share = cols // n
    vmem = pl.BlockSpec(memory_space=pltpu.VMEM)
    hbm = pl.BlockSpec(memory_space=pltpu.HBM)
    unread = pl.BlockSpec(memory_space=pl.ANY)

    def far(*arrays):
        return [pltpu.with_memory_space_constraint(x, pltpu.HBM) for x in arrays]

    def like(array):
        return pltpu.VMEM(array.shape, array.dtype)

    def swap(array, axis, k):
        size = {"aa": groups, "ba": n}[axis]
        return lax.ppermute(array, axis, [(i, i ^ k) for i in range(size)])

    sizes = [share + rank * (2 + len(partners(n, k))) for k in range(1, n)] + [share + rank * (n + 1)]
    *messages, own, sides_held, inverse_held, gather, pair, top_held, order_held = call(
        functools.partial(front_kernel, n),
        [shape((size, rank)) for size in sizes]
        + [shape(sides.shape), shape(inverse.shape)]
        + [shape((points, points)), shape((points, 2 * rank)), shape(top.shape), shape(order.shape, order.dtype)],
        [hbm] * 8,
        scratch=[like(x) for x in (skel, basis, core, transfer)]
        + [pltpu.VMEM((cols, rank), BF), pltpu.SemaphoreType.DMA((7 + PIECES,))],
        flops=2 * rank * points * (3 * points + cols),
        moved=2 * points * (points + cols + rank),
    )(*far(order, skel, sides, inverse, basis, core, transfer, top))
    received = [swap(messages[k - 1], "ba", k) for k in range(1, n)]
    ordered, top_held = call(
        ordered_kernel,
        [shape((points, cols)), shape(top.shape)],
        [vmem] * 3,
        flops=2 * points * points * cols,
        moved=2 * points * (points + 2 * cols),
    )(sides_held, gather, top_held)
    tops = [top_held] + [swap(top_held, "ba", k) for k in range(1, n)]
    level, group = call(
        functools.partial(group_kernel, n, rank),
        [shape((share, n * rank), F32), shape((share, rank))],
        [unread] + [vmem] * n,
        flops=2 * share * n * rank * (n + 1) * rank,
        moved=4 * share * n * rank,
    )(ordered, own, *received[::-1])
    applied, group_held = call(
        applied_kernel,
        [shape((points, cols)), shape((share, rank))],
        [vmem] * 3,
        flops=2 * points * points * cols,
        moved=2 * points * (points + 2 * cols),
    )(inverse_held, ordered, group)
    pieces = {0: group}
    for m in range(2, groups, 2):
        pieces[m] = swap(group, "aa", m)
    for m in range(0, groups, 2):
        pieces[m + 1] = swap(pieces[m] if m else group_held, "aa", 1)
    rows = call(
        functools.partial(top_rows_kernel, n, groups),
        shape((rank, groups * rank)),
        [vmem] * n,
        scratch=[pltpu.VMEM((rank, groups * rank), F32)],
        moved=4 * rank * groups * rank,
    )(*tops[::-1])
    corrections = call(
        functools.partial(top_kernel, n, groups),
        [shape((share, rank))] * n,
        [vmem] * (2 + n + groups),
        flops=2 * share * rank * (groups + n) * rank,
        moved=4 * share * n * rank,
    )(rows, level, own, *received, *[pieces[m] for m in range(groups)])
    back = [corrections[0]] + [swap(corrections[k], "ba", k) for k in range(1, n)]
    applied, down = call(
        down_kernel,
        [shape((points, cols)), shape((points, rank))],
        [vmem] * 4 + [unread],
        flops=2 * points * points * (3 * rank + cols),
        moved=2 * points * (points + 2 * cols),
    )(inverse_held, order_held, pair, applied, corrections[0])
    return call(
        functools.partial(final_kernel, n),
        shape((points, cols)),
        [vmem] * (2 + n),
        out_specs=hbm,
        scratch=[pltpu.VMEM((cols, rank), BF), pltpu.VMEM((points, cols), BF), pltpu.SemaphoreType.DMA((PIECES,))],
        flops=2 * points * cols * rank,
        moved=4 * points * cols,
    )(applied, down, *back[::-1])


def solution(mesh):
    spec = P(("aa", "ba"), None)
    return jax.shard_map(
        functools.partial(shards, mesh.shape["ba"], mesh.shape["aa"]),
        mesh=mesh,
        in_specs=(spec,) * 8,
        out_specs=spec,
        check_vma=False,
    )
```

```python
import functools

import jax
import jax.numpy as jnp
from jax import lax
from jax.experimental import pallas as pl
from jax.experimental.pallas import tpu as pltpu
from jax.sharding import PartitionSpec as P

BF = jnp.bfloat16
F32 = jnp.float32
NN = (((1,), (0,)), ((), ()))
NT = (((1,), (1,)), ((), ()))
TN = (((0,), (0,)), ((), ()))


def dot(a, b, dims=NN):
    return lax.dot_general(a, b, dims, preferred_element_type=F32)


def partners(n, k):
    return [m for m in range(1, n) if (m.bit_count(), -m) > (k.bit_count(), -k)]


def column_of(row, count):
    wide = jnp.broadcast_to(row.astype(F32), (count, row.shape[1]))
    return wide.T.astype(jnp.int32)


def order_rows(order, size):
    return jnp.where(
        lax.broadcasted_iota(jnp.int32, (size, size), 0) == order, 1.0, 0.0
    ).astype(BF)


def order_columns(order, size):
    column = column_of(order, 128)
    lanes = lax.broadcasted_iota(jnp.int32, (size, 128), 1)
    return jnp.concatenate(
        [jnp.where(column == lanes + j * 128, 1.0, 0.0).astype(BF) for j in range(size // 128)], axis=1
    )


def basis_pair(skel, basis):
    points, rank = basis.shape
    ones = jnp.where(
        lax.broadcasted_iota(jnp.int32, (points, rank), 0) == skel, 1.0, 0.0
    ).astype(BF)
    return jnp.concatenate([basis, ones], axis=1)


def fetch(sources, sems):
    copies = [pltpu.make_async_copy(src, dst, sems.at[j]) for j, (src, dst) in enumerate(sources)]
    for copy in copies:
        copy.start()
    return copies


def pieces_of(ref, count):
    rows = ref.shape[0] // count
    return [ref.at[pl.ds(j * rows, rows)] for j in range(count)]


PIECES = 4


def front_kernel(
    n, order_hbm, skel_hbm, sides_hbm, inverse_hbm, basis_hbm, core_hbm, transfer_hbm, top_hbm, *rest
):
    messages, own_ref = rest[: n - 1], rest[n - 1]
    sides_ref, inverse_ref, gather_ref, pair_ref, top_ref, order_ref = rest[n : n + 6]
    skel_ref, basis_ref, core_ref, transfer_ref, coeffs, sems = rest[n + 6 :]
    me = lax.axis_index("ba")
    points, rank = basis_ref.shape
    rows = points // PIECES
    copies = fetch(
        [(skel_hbm, skel_ref), (basis_hbm, basis_ref), (order_hbm, order_ref)]
        + list(zip(pieces_of(inverse_hbm, PIECES), pieces_of(inverse_ref, PIECES)))
        + [(sides_hbm, sides_ref), (core_hbm, core_ref), (transfer_hbm, transfer_ref), (top_hbm, top_ref)],
        sems,
    )
    share = coeffs.shape[0] // n
    for copy in copies[:3]:
        copy.wait()
    pair_ref[...] = basis_pair(skel_ref[...], basis_ref[...])
    gather_ref[...] = order_columns(order_ref[...], points)
    both = None
    for j in range(PIECES):
        copies[3 + j].wait()
        at = slice(j * rows, (j + 1) * rows)
        part = dot(pair_ref[at, :], inverse_ref[at, :], TN)
        both = part if both is None else both + part
    up = (both[:rank] + both[rank:]).astype(BF)
    up = dot(up, gather_ref[...]).astype(BF)
    for copy in copies[3 + PIECES :]:
        copy.wait()
    coeffs[...] = dot(up, sides_ref[...]).T.astype(BF)
    transfer = transfer_ref[...].astype(BF)

    def block(m):
        return core_ref[:, pl.ds(pl.multiple_of((me ^ m) * rank, rank), rank)]

    for k in range(n):
        out = own_ref if k == 0 else messages[k - 1]
        out[0:share, :] = coeffs[pl.ds(pl.multiple_of((me ^ k) * share, share), share), :]
        out[share : share + rank, :] = transfer
        at = share + rank
        for m in range(n) if k == 0 else [0] + [k ^ m for m in partners(n, k)]:
            out[at : at + rank, :] = block(m)
            at += rank


def applied_kernel(sides_ref, inverse_ref, gather_ref, top_ref, applied_ref, top_out):
    ordered = dot(gather_ref[...], sides_ref[...]).astype(BF)
    applied_ref[...] = dot(inverse_ref[...], ordered).astype(BF)
    top_out[...] = top_ref[...]


def down_kernel(inverse_ref, order_ref, pair_ref, applied_ref, after, applied_out, down_ref):
    del after
    points, rank = down_ref.shape
    placed = order_rows(order_ref[...], points)
    both = dot(inverse_ref[...], pair_ref[...])
    down = (both[:, :rank] + both[:, rank:]).astype(BF)
    applied_out[...] = dot(placed, applied_ref[...]).astype(BF)
    down_ref[...] = dot(placed, down).astype(BF)


def group_kernel(n, rank, after, own_ref, *rest):
    del after
    messages, (level_ref, group_ref) = rest[: n - 1], rest[n - 1 :]
    share = level_ref.shape[0]
    messages = messages[::-1]
    coeffs = [msg[0:share, :] for msg in (own_ref,) + messages]
    transfers = [msg[share : share + rank, :] for msg in (own_ref,) + messages]
    level = [None] * n

    def add(k, term):
        level[k] = term if level[k] is None else level[k] + term

    for k in range(n):
        msg = own_ref if k == 0 else messages[k - 1]
        which = list(range(n)) if k == 0 else [k] + partners(n, k)
        blocks = [msg[share + rank * (j + 1) : share + rank * (j + 2), :] for j in range(len(which))]
        wide = dot(coeffs[k], jnp.concatenate(blocks, axis=1))
        for j, m in enumerate(which):
            add(m, wide[:, j * rank : (j + 1) * rank])
        if len(which) > 1:
            others = jnp.concatenate([coeffs[m] for m in which[1:]], axis=1)
            add(k, dot(others, jnp.concatenate(blocks[1:], axis=1), NT))
    level_ref[...] = jnp.concatenate(level, axis=1)
    rest_of = [(coeffs[k].astype(F32) - level[k]).astype(BF) for k in range(n)]
    total = dot(jnp.concatenate(rest_of, axis=1), jnp.concatenate(transfers, axis=0))
    group_ref[...] = total.astype(BF)


def top_rows_kernel(n, groups, *rest):
    tops, (rows_ref, held) = rest[:n], rest[n:]
    me = lax.axis_index("ba")
    mine = lax.axis_index("aa")
    part = tops[0].shape[0]
    rank = rows_ref.shape[0]
    for k in range(n):
        held[pl.ds(pl.multiple_of((me ^ k) * part, part), part), :] = tops[k][...].astype(F32)
    for m in range(groups):
        rows_ref[:, m * rank : (m + 1) * rank] = held[
            :, pl.ds(pl.multiple_of((mine ^ m) * rank, rank), rank)
        ].astype(BF)


def top_kernel(n, groups, rows_ref, level_ref, *rest):
    messages, pieces, outs = rest[:n], rest[n : n + groups], rest[n + groups :]
    share = level_ref.shape[0]
    rank = rows_ref.shape[0]
    stacked = jnp.concatenate([piece[...] for piece in pieces], axis=1)
    top = dot(stacked, rows_ref[...], NT).astype(BF)
    transfers = jnp.concatenate([msg[share : share + rank, :] for msg in messages], axis=0)
    correction = (level_ref[...] + dot(top, transfers, NT)).astype(BF)
    for k in range(n):
        outs[k][...] = correction[:, k * rank : (k + 1) * rank]


def final_kernel(n, applied_ref, down_ref, *rest):
    pieces, (out_hbm, correction, out_ref, sems) = rest[:n][::-1], rest[n:]
    me = lax.axis_index("ba")
    share = pieces[0].shape[0]
    for k in range(n):
        correction[pl.ds(pl.multiple_of((me ^ k) * share, share), share), :] = pieces[k][...]
    rows = out_ref.shape[0] // PIECES
    copies = []
    for j, (src, dst) in enumerate(zip(pieces_of(out_ref, PIECES), pieces_of(out_hbm, PIECES))):
        at = slice(j * rows, (j + 1) * rows)
        out_ref[at, :] = (
            applied_ref[at, :].astype(F32) - dot(down_ref[at, :], correction[...], NT)
        ).astype(BF)
        copies.append(pltpu.make_async_copy(src, dst, sems.at[j]))
        copies[-1].start()
    for copy in copies:
        copy.wait()


def shape(dims, kind=BF):
    return jax.ShapeDtypeStruct(dims, kind)


def call(body, outs, in_specs, out_specs=None, scratch=(), flops=0, moved=0, limit=32):
    return pl.pallas_call(
        body,
        out_shape=outs,
        in_specs=in_specs,
        scratch_shapes=list(scratch),
        compiler_params=pltpu.CompilerParams(vmem_limit_bytes=limit * 1024 * 1024),
        cost_estimate=pl.CostEstimate(flops=flops, bytes_accessed=moved, transcendentals=0),
        **({} if out_specs is None else {"out_specs": out_specs}),
    )


def shards(n, groups, sides, order, skel, inverse, basis, core, transfer, top):
    points, cols = sides.shape
    rank = basis.shape[1]
    share = cols // n
    vmem = pl.BlockSpec(memory_space=pltpu.VMEM)
    hbm = pl.BlockSpec(memory_space=pltpu.HBM)
    unread = pl.BlockSpec(memory_space=pl.ANY)

    def far(*arrays):
        return [pltpu.with_memory_space_constraint(x, pltpu.HBM) for x in arrays]

    def like(array):
        return pltpu.VMEM(array.shape, array.dtype)

    def swap(array, axis, k):
        size = {"aa": groups, "ba": n}[axis]
        return lax.ppermute(array, axis, [(i, i ^ k) for i in range(size)])

    sizes = [share + rank * (2 + len(partners(n, k))) for k in range(1, n)] + [share + rank * (n + 1)]
    *messages, own, sides_held, inverse_held, gather, pair, top_held, order_held = call(
        functools.partial(front_kernel, n),
        [shape((size, rank)) for size in sizes]
        + [shape(sides.shape), shape(inverse.shape)]
        + [shape((points, points)), shape((points, 2 * rank)), shape(top.shape), shape(order.shape, order.dtype)],
        [hbm] * 8,
        scratch=[like(x) for x in (skel, basis, core, transfer)]
        + [pltpu.VMEM((cols, rank), BF), pltpu.SemaphoreType.DMA((7 + PIECES,))],
        flops=2 * rank * points * (3 * points + cols),
        moved=2 * points * (points + cols + rank),
    )(*far(order, skel, sides, inverse, basis, core, transfer, top))
    received = [swap(messages[k - 1], "ba", k) for k in range(1, n)]
    applied, top_held = call(
        applied_kernel,
        [shape((points, cols)), shape(top.shape)],
        [vmem] * 4,
        flops=4 * points * points * cols,
        moved=2 * points * (points + 2 * cols),
    )(sides_held, inverse_held, gather, top_held)
    tops = [top_held] + [swap(top_held, "ba", k) for k in range(1, n)]
    level, group = call(
        functools.partial(group_kernel, n, rank),
        [shape((share, n * rank), F32), shape((share, rank))],
        [unread] + [vmem] * n,
        flops=2 * share * n * rank * (n + 1) * rank,
        moved=4 * share * n * rank,
    )(applied, own, *received[::-1])
    pieces = {0: group}
    for m in range(2, groups, 2):
        pieces[m] = swap(group, "aa", m)
    for m in range(0, groups, 2):
        pieces[m + 1] = swap(pieces[m], "aa", 1)
    rows = call(
        functools.partial(top_rows_kernel, n, groups),
        shape((rank, groups * rank)),
        [vmem] * n,
        scratch=[pltpu.VMEM((rank, groups * rank), F32)],
        moved=4 * rank * groups * rank,
    )(*tops)
    corrections = call(
        functools.partial(top_kernel, n, groups),
        [shape((share, rank))] * n,
        [vmem] * (2 + n + groups),
        flops=2 * share * rank * (groups + n) * rank,
        moved=4 * share * n * rank,
    )(rows, level, own, *received, *[pieces[m] for m in range(groups)])
    back = [corrections[0]] + [swap(corrections[k], "ba", k) for k in range(1, n)]
    applied, down = call(
        down_kernel,
        [shape((points, cols)), shape((points, rank))],
        [vmem] * 4 + [unread],
        flops=2 * points * points * (3 * rank + cols),
        moved=2 * points * (points + 2 * cols),
    )(inverse_held, order_held, pair, applied, corrections[0])
    return call(
        functools.partial(final_kernel, n),
        shape((points, cols)),
        [vmem] * (2 + n),
        out_specs=hbm,
        scratch=[pltpu.VMEM((cols, rank), BF), pltpu.VMEM((points, cols), BF), pltpu.SemaphoreType.DMA((PIECES,))],
        flops=2 * points * cols * rank,
        moved=4 * points * cols,
    )(applied, down, *back[::-1])


def solution(mesh):
    spec = P(("aa", "ba"), None)
    return jax.shard_map(
        functools.partial(shards, mesh.shape["ba"], mesh.shape["aa"]),
        mesh=mesh,
        in_specs=(spec,) * 8,
        out_specs=spec,
        check_vma=False,
    )
```

```python
import functools

import jax
import jax.numpy as jnp
from jax import lax
from jax.experimental import pallas as pl
from jax.experimental.pallas import tpu as pltpu
from jax.sharding import PartitionSpec as P

BF = jnp.bfloat16
F32 = jnp.float32
NN = (((1,), (0,)), ((), ()))
NT = (((1,), (1,)), ((), ()))
TN = (((0,), (0,)), ((), ()))


def dot(a, b, dims=NN):
    return lax.dot_general(a, b, dims, preferred_element_type=F32)


def partners(n, k):
    half = (n - 2) // 2
    return [(k - 1 + j) % (n - 1) + 1 for j in range(1, half + 1)]


def column_of(row, count):
    wide = jnp.broadcast_to(row.astype(F32), (count, row.shape[1]))
    return wide.T.astype(jnp.int32)


def order_rows(order, size):
    return jnp.where(
        lax.broadcasted_iota(jnp.int32, (size, size), 0) == order, 1.0, 0.0
    ).astype(BF)


def order_columns(order, size):
    column = column_of(order, 128)
    lanes = lax.broadcasted_iota(jnp.int32, (size, 128), 1)
    return jnp.concatenate(
        [jnp.where(column == lanes + j * 128, 1.0, 0.0).astype(BF) for j in range(size // 128)], axis=1
    )


def basis_pair(skel, basis):
    points, rank = basis.shape
    ones = jnp.where(
        lax.broadcasted_iota(jnp.int32, (points, rank), 0) == skel, 1.0, 0.0
    ).astype(BF)
    return jnp.concatenate([basis, ones], axis=1)


def fetch(sources, sems):
    copies = [pltpu.make_async_copy(src, dst, sems.at[j]) for j, (src, dst) in enumerate(sources)]
    for copy in copies:
        copy.start()
    return copies


def pieces_of(ref, count):
    rows = ref.shape[0] // count
    return [ref.at[pl.ds(j * rows, rows)] for j in range(count)]


PIECES = 4


def front_kernel(
    n, order_hbm, skel_hbm, sides_hbm, inverse_hbm, basis_hbm, core_hbm, transfer_hbm, top_hbm, *rest
):
    messages, own_ref = rest[: n - 1], rest[n - 1]
    sides_ref, inverse_ref, gather_ref, pair_ref, top_ref, order_ref = rest[n : n + 6]
    skel_ref, basis_ref, core_ref, transfer_ref, coeffs, sems = rest[n + 6 :]
    me = lax.axis_index("ba")
    points, rank = basis_ref.shape
    rows = points // PIECES
    copies = fetch(
        [(skel_hbm, skel_ref), (basis_hbm, basis_ref), (order_hbm, order_ref)]
        + list(zip(pieces_of(inverse_hbm, PIECES), pieces_of(inverse_ref, PIECES)))
        + [(sides_hbm, sides_ref), (core_hbm, core_ref), (transfer_hbm, transfer_ref), (top_hbm, top_ref)],
        sems,
    )
    share = coeffs.shape[0] // n
    for copy in copies[:3]:
        copy.wait()
    pair_ref[...] = basis_pair(skel_ref[...], basis_ref[...])
    gather_ref[...] = order_columns(order_ref[...], points)
    both = None
    for j in range(PIECES):
        copies[3 + j].wait()
        at = slice(j * rows, (j + 1) * rows)
        part = dot(pair_ref[at, :], inverse_ref[at, :], TN)
        both = part if both is None else both + part
    up = (both[:rank] + both[rank:]).astype(BF)
    up = dot(up, gather_ref[...]).astype(BF)
    for copy in copies[3 + PIECES :]:
        copy.wait()
    coeffs[...] = dot(up, sides_ref[...]).T.astype(BF)
    transfer = transfer_ref[...].astype(BF)

    def block(m):
        return core_ref[:, pl.ds(pl.multiple_of((me ^ m) * rank, rank), rank)]

    for k in range(n):
        out = own_ref if k == 0 else messages[k - 1]
        out[0:share, :] = coeffs[pl.ds(pl.multiple_of((me ^ k) * share, share), share), :]
        out[share : share + rank, :] = transfer
        at = share + rank
        for m in range(n) if k == 0 else [0] + [k ^ m for m in partners(n, k)]:
            out[at : at + rank, :] = block(m)
            at += rank


def applied_kernel(sides_ref, inverse_ref, gather_ref, top_ref, applied_ref, top_out):
    ordered = dot(gather_ref[...], sides_ref[...]).astype(BF)
    applied_ref[...] = dot(inverse_ref[...], ordered).astype(BF)
    top_out[...] = top_ref[...]


def down_kernel(inverse_ref, pair_ref, group_ref, down_ref, group_out):
    rank = down_ref.shape[1]
    both = dot(inverse_ref[...], pair_ref[...])
    down_ref[...] = (both[:, :rank] + both[:, rank:]).astype(BF)
    group_out[...] = group_ref[...]


def place_kernel(order_ref, applied_ref, down_ref, after, applied_out, down_out):
    del after
    placed = order_rows(order_ref[...], applied_ref.shape[0])
    applied_out[...] = dot(placed, applied_ref[...]).astype(BF)
    down_out[...] = dot(placed, down_ref[...]).astype(BF)


def group_kernel(n, rank, after, own_ref, *rest):
    del after
    messages, (level_ref, group_ref) = rest[: n - 1], rest[n - 1 :]
    share = level_ref.shape[0]
    messages = messages[::-1]
    coeffs = [msg[0:share, :] for msg in (own_ref,) + messages]
    transfers = [msg[share : share + rank, :] for msg in (own_ref,) + messages]
    level = [None] * n

    def add(k, term):
        level[k] = term if level[k] is None else level[k] + term

    for k in range(n):
        msg = own_ref if k == 0 else messages[k - 1]
        which = list(range(n)) if k == 0 else [k] + partners(n, k)
        blocks = [msg[share + rank * (j + 1) : share + rank * (j + 2), :] for j in range(len(which))]
        wide = dot(coeffs[k], jnp.concatenate(blocks, axis=1))
        for j, m in enumerate(which):
            add(m, wide[:, j * rank : (j + 1) * rank])
        if len(which) > 1:
            others = jnp.concatenate([coeffs[m] for m in which[1:]], axis=1)
            add(k, dot(others, jnp.concatenate(blocks[1:], axis=1), NT))
    level_ref[...] = jnp.concatenate(level, axis=1)
    rest_of = [(coeffs[k].astype(F32) - level[k]).astype(BF) for k in range(n)]
    total = dot(jnp.concatenate(rest_of, axis=1), jnp.concatenate(transfers, axis=0))
    group_ref[...] = total.astype(BF)


def top_rows_kernel(n, groups, *rest):
    tops, (rows_ref, held) = rest[:n], rest[n:]
    me = lax.axis_index("ba")
    mine = lax.axis_index("aa")
    part = tops[0].shape[0]
    rank = rows_ref.shape[0]
    for k in range(n):
        held[pl.ds(pl.multiple_of((me ^ k) * part, part), part), :] = tops[k][...].astype(F32)
    for m in range(groups):
        rows_ref[:, m * rank : (m + 1) * rank] = held[
            :, pl.ds(pl.multiple_of((mine ^ m) * rank, rank), rank)
        ].astype(BF)


def top_kernel(n, groups, rows_ref, level_ref, *rest):
    messages, pieces, outs = rest[:n], rest[n : n + groups], rest[n + groups :]
    share = level_ref.shape[0]
    rank = rows_ref.shape[0]
    stacked = jnp.concatenate([piece[...] for piece in pieces], axis=1)
    top = dot(stacked, rows_ref[...], NT).astype(BF)
    transfers = jnp.concatenate([msg[share : share + rank, :] for msg in messages], axis=0)
    correction = (level_ref[...] + dot(top, transfers, NT)).astype(BF)
    for k in range(n):
        outs[k][...] = correction[:, k * rank : (k + 1) * rank]


def final_kernel(n, applied_ref, down_ref, *rest):
    pieces, (out_hbm, correction, out_ref, sems) = rest[:n][::-1], rest[n:]
    me = lax.axis_index("ba")
    share = pieces[0].shape[0]
    for k in range(n):
        correction[pl.ds(pl.multiple_of((me ^ k) * share, share), share), :] = pieces[k][...]
    rows = out_ref.shape[0] // PIECES
    copies = []
    for j, (src, dst) in enumerate(zip(pieces_of(out_ref, PIECES), pieces_of(out_hbm, PIECES))):
        at = slice(j * rows, (j + 1) * rows)
        out_ref[at, :] = (
            applied_ref[at, :].astype(F32) - dot(down_ref[at, :], correction[...], NT)
        ).astype(BF)
        copies.append(pltpu.make_async_copy(src, dst, sems.at[j]))
        copies[-1].start()
    for copy in copies:
        copy.wait()


def shape(dims, kind=BF):
    return jax.ShapeDtypeStruct(dims, kind)


def call(body, outs, in_specs, out_specs=None, scratch=(), flops=0, moved=0, limit=32):
    return pl.pallas_call(
        body,
        out_shape=outs,
        in_specs=in_specs,
        scratch_shapes=list(scratch),
        compiler_params=pltpu.CompilerParams(vmem_limit_bytes=limit * 1024 * 1024),
        cost_estimate=pl.CostEstimate(flops=flops, bytes_accessed=moved, transcendentals=0),
        **({} if out_specs is None else {"out_specs": out_specs}),
    )


def shards(n, groups, sides, order, skel, inverse, basis, core, transfer, top):
    points, cols = sides.shape
    rank = basis.shape[1]
    share = cols // n
    vmem = pl.BlockSpec(memory_space=pltpu.VMEM)
    hbm = pl.BlockSpec(memory_space=pltpu.HBM)
    unread = pl.BlockSpec(memory_space=pl.ANY)

    def far(*arrays):
        return [pltpu.with_memory_space_constraint(x, pltpu.HBM) for x in arrays]

    def like(array):
        return pltpu.VMEM(array.shape, array.dtype)

    def swap(array, axis, k):
        size = {"aa": groups, "ba": n}[axis]
        return lax.ppermute(array, axis, [(i, i ^ k) for i in range(size)])

    sizes = [share + rank * (2 + len(partners(n, k))) for k in range(1, n)] + [share + rank * (n + 1)]
    *messages, own, sides_held, inverse_held, gather, pair, top_held, order_held = call(
        functools.partial(front_kernel, n),
        [shape((size, rank)) for size in sizes]
        + [shape(sides.shape), shape(inverse.shape)]
        + [shape((points, points)), shape((points, 2 * rank)), shape(top.shape), shape(order.shape, order.dtype)],
        [hbm] * 8,
        scratch=[like(x) for x in (skel, basis, core, transfer)]
        + [pltpu.VMEM((cols, rank), BF), pltpu.SemaphoreType.DMA((7 + PIECES,))],
        flops=2 * rank * points * (3 * points + cols),
        moved=2 * points * (points + cols + rank),
    )(*far(order, skel, sides, inverse, basis, core, transfer, top))
    received = [swap(messages[k - 1], "ba", k) for k in range(1, n)]
    applied, top_held = call(
        applied_kernel,
        [shape((points, cols)), shape(top.shape)],
        [vmem] * 4,
        flops=4 * points * points * cols,
        moved=2 * points * (points + 2 * cols),
    )(sides_held, inverse_held, gather, top_held)
    tops = [top_held] + [swap(top_held, "ba", k) for k in range(1, n)]
    level, group = call(
        functools.partial(group_kernel, n, rank),
        [shape((share, n * rank), F32), shape((share, rank))],
        [unread] + [vmem] * n,
        flops=2 * share * n * rank * (n + 1) * rank,
        moved=4 * share * n * rank,
    )(applied, own, *received[::-1])
    down, group_held = call(
        down_kernel,
        [shape((points, rank)), shape((share, rank))],
        [vmem] * 3,
        flops=4 * points * points * rank,
        moved=2 * points * (points + 2 * rank),
    )(inverse_held, pair, group)
    pieces = {0: group}
    for m in range(2, groups, 2):
        pieces[m] = swap(group, "aa", m)
    for m in range(0, groups, 2):
        pieces[m + 1] = swap(pieces[m] if m else group_held, "aa", 1)
    rows = call(
        functools.partial(top_rows_kernel, n, groups),
        shape((rank, groups * rank)),
        [vmem] * n,
        scratch=[pltpu.VMEM((rank, groups * rank), F32)],
        moved=4 * rank * groups * rank,
    )(*tops)
    corrections = call(
        functools.partial(top_kernel, n, groups),
        [shape((share, rank))] * n,
        [vmem] * (2 + n + groups),
        flops=2 * share * rank * (groups + n) * rank,
        moved=4 * share * n * rank,
    )(rows, level, own, *received, *[pieces[m] for m in range(groups)])
    back = [corrections[0]] + [swap(corrections[k], "ba", k) for k in range(1, n)]
    applied, down = call(
        place_kernel,
        [shape((points, cols)), shape((points, rank))],
        [vmem] * 3 + [unread],
        flops=2 * points * points * (rank + cols),
        moved=2 * points * (points + 2 * cols),
    )(order_held, applied, down, corrections[0])
    return call(
        functools.partial(final_kernel, n),
        shape((points, cols)),
        [vmem] * (2 + n),
        out_specs=hbm,
        scratch=[pltpu.VMEM((cols, rank), BF), pltpu.VMEM((points, cols), BF), pltpu.SemaphoreType.DMA((PIECES,))],
        flops=2 * points * cols * rank,
        moved=4 * points * cols,
    )(applied, down, *back[::-1])


def solution(mesh):
    spec = P(("aa", "ba"), None)
    return jax.shard_map(
        functools.partial(shards, mesh.shape["ba"], mesh.shape["aa"]),
        mesh=mesh,
        in_specs=(spec,) * 8,
        out_specs=spec,
        check_vma=False,
    )
```
